32 devices in a mesh: seq: 8 (over y, x, core), head: 4 (over z).
Axes of the slice: x: 2, y: 2, z: 4, core: 2. Of those that a mesh axis runs over, the one named last changes fastest.
Arguments:
- tokens: bfloat16 [2, 4096, 1024], P(None, 'seq'), may hold values from -6 to 6
- cotangent: bfloat16 [2, 4096, 1024], P(None, 'seq'), may hold values from -6 to 6
- doc_starts: int32 [2, 4], replicated, may hold values from 0 to 4096, as said below
- norm_gain: float32 [1024], replicated, may hold values from 0.5 to 1.5
- mixer_proj: bfloat16 [1024, 2, 1536], P(None, None, 'head'), may hold values from -0.1875 to 0.1875
- state_proj: bfloat16 [1024, 256], replicated, may hold values from -0.1875 to 0.1875
- step_proj: bfloat16 [1024, 24], P(None, 'head'), may hold values from -0.1875 to 0.1875
- step_bias: float32 [24], P('head'), may hold values from -2 to 0
- decay_log: float32 [24], P('head'), as said below
- skip_gain: float32 [24], P('head'), may hold values from 0.5 to 1.5
- conv_mixer: float32 [4, 1536], P(None, 'head'), may hold values from -3 to 3
- conv_state: float32 [4, 256], replicated, may hold values from -0.75 to 0.75
- mixer_down: bfloat16 [1536, 1024], P('head'), may hold values from -0.15625 to 0.15625
- query_proj: bfloat16 [1024, 512], P(None, 'head'), may hold values from -0.1875 to 0.1875
- keyval_proj: bfloat16 [1024, 2, 128], replicated, may hold values from -0.1875 to 0.1875
- attend_down: bfloat16 [512, 1024], P('head'), may hold values from -3 to 3
- ffn_gain: float32 [1024], replicated, may hold values from 0.5 to 1.5
- ffn_in: bfloat16 [1024, 2, 2048], P(None, None, 'head'), may hold values from -0.1875 to 0.1875
- ffn_down: bfloat16 [2048, 1024], P('head'), may hold values from -0.125 to 0.125
Outputs:
- output: bfloat16 [2, 4096, 1024], P(None, 'seq')
- token_grad: bfloat16 [2, 4096, 1024], P(None, 'seq')
- norm_gain_grad: float32 [1024], replicated
- mixer_proj_grad: float32 [1024, 2, 1536], P(None, None, 'head')
- state_proj_grad: float32 [1024, 256], replicated
- step_proj_grad: float32 [1024, 24], P(None, 'head')
- step_bias_grad: float32 [24], P('head')
- decay_log_grad: float32 [24], P('head')
- skip_gain_grad: float32 [24], P('head')
- conv_mixer_grad: float32 [4, 1536], P(None, 'head')
- conv_state_grad: float32 [4, 256], replicated
- mixer_down_grad: float32 [1536, 1024], P('head')
- query_proj_grad: float32 [1024, 512], P(None, 'head')
- keyval_proj_grad: float32 [1024, 2, 128], replicated
- attend_down_grad: float32 [512, 1024], P('head')
- ffn_gain_grad: float32 [1024], replicated
- ffn_in_grad: float32 [1024, 2, 2048], P(None, None, 'head')
- ffn_down_grad: float32 [2048, 1024], P('head')
The draws below stay inside these ranges and needn't reach their ends.
Inputs may be any that keep to these rules, and one draw needn't show every extreme that they name: `doc_starts`: each row lists its documents' first places in rising order, the first 0; a start equal to 4096 is an empty document. In one row, drawn from the seed, a single document fills the whole row; the other rows hold 4 documents, none empty. `decay_log`: each head's value lies between ln(0.02 / 4096) and ln(1 / 16).
All inputs are finite; a program needn't handle non-finite values.
Results may differ from the reference program's by a relative error of at most 0.029.
Values may be sent and summed in bfloat16 or wider, within the bound.
A program may use at most 192 MiB of HBM per device.

```python
import math
import jax
import jax.numpy as jnp
from jax import lax

D = 1024
SSM_HEADS = 24
SSM_DIM = 64
STATE = 128
CONV = 4
ATT_HEADS = 8
KV_HEADS = 2
ATT_DIM = 64
FF = 2048
ROWS = 2
CH = 512
DOCS = 4
LEN = 4096


def draw_doc_starts(key, part):
    key = jax.random.fold_in(key, 5)
    pick_key, cut_key = jax.random.split(key)
    whole_row = jax.random.randint(pick_key, (), 0, ROWS)
    row_keys = jax.random.split(cut_key, ROWS)

    def row_starts(row_key):
        cuts = jax.random.choice(row_key, LEN - 1, (DOCS - 1,), replace=False) + 1
        return jnp.concatenate([jnp.zeros((1,), jnp.int32), jnp.sort(cuts).astype(jnp.int32)])
    ragged = jax.vmap(row_starts)(row_keys)
    single = jnp.concatenate([jnp.zeros((1,), jnp.int32), jnp.full((DOCS - 1,), LEN, jnp.int32)])
    return jnp.where((jnp.arange(ROWS) == whole_row)[:, None], single[None, :], ragged)


def draw_decay_log(key, part):
    key = jax.random.fold_in(key, 9)
    lowest = math.log(0.02 / LEN)
    highest = math.log(1.0 / 16)
    return jax.random.uniform(key, (SSM_HEADS,), jnp.float32, lowest, highest)


def level_of(rng, dims, pieces, smallest, top_value):
    level, own = 1.0, jax.random.fold_in(rng, 6)
    for dim, shards_of in pieces:
        draws = jnp.exp(jax.random.uniform(jax.random.fold_in(own, dim), (shards_of,), jnp.float32, smallest / len(pieces), top_value / len(pieces)))
        level = level * jnp.repeat(draws, dims[dim] // shards_of).reshape([-1 if axis == dim else 1 for axis in range(len(dims))])
    return level


def noise(stream_key, dims, width, bound, cuts=(), held_as=jnp.bfloat16):
    values = width * jax.random.normal(stream_key, dims, jnp.float32)
    if cuts:
        values = values * level_of(stream_key, dims, cuts, -0.22, 0.18)
    return jnp.clip(values, -bound, bound).astype(held_as)


def setup_inputs(seed: int = 0) -> dict:
    streams_of = jax.random.split(jax.random.key(seed), 20)
    tokens = noise(streams_of[0], (ROWS, LEN, D), 1.0, 6.0, ((1, 8),))
    cotangent = noise(streams_of[1], (ROWS, LEN, D), 1.0, 6.0, ((1, 8),))
    doc_starts = draw_doc_starts(jax.random.fold_in(streams_of[19], 71), 0)
    norm_gain = jnp.clip(1.0 + 0.1 * jax.random.normal(streams_of[3], (D,), jnp.float32), 0.5, 1.5)
    mixer_proj = noise(streams_of[4], (D, 2, SSM_HEADS * SSM_DIM), D ** -0.5, 0.1875, ((2, 4),))
    state_proj = noise(streams_of[5], (D, 2 * STATE), D ** -0.5, 0.1875)
    step_proj = noise(streams_of[6], (D, SSM_HEADS), D ** -0.5, 0.1875, ((1, 4),))
    step_bias = jnp.clip(-2.0 + 2.0 * jax.random.uniform(streams_of[7], (SSM_HEADS,), jnp.float32) ** level_of(streams_of[7], (SSM_HEADS,), ((0, 4),), -0.2, 0.2), -2.0, 0.0)
    decay_log = draw_decay_log(jax.random.fold_in(streams_of[19], 71), 0)
    skip_gain = jnp.clip(0.5 + 1.0 * jax.random.uniform(streams_of[9], (SSM_HEADS,), jnp.float32) ** level_of(streams_of[9], (SSM_HEADS,), ((0, 4),), -0.2, 0.2), 0.5, 1.5)
    conv_mixer = noise(streams_of[10], (CONV, SSM_HEADS * SSM_DIM), CONV ** -0.5, 3.0, ((1, 4),), jnp.float32)
    conv_state = noise(streams_of[11], (CONV, 2 * STATE), (16 * CONV) ** -0.5, 0.75, (), jnp.float32)
    mixer_down = noise(streams_of[12], (SSM_HEADS * SSM_DIM, D), (SSM_HEADS * SSM_DIM) ** -0.5, 0.15625, ((0, 4),))
    query_proj = noise(streams_of[13], (D, ATT_HEADS * ATT_DIM), D ** -0.5, 0.1875, ((1, 4),))
    keyval_proj = noise(streams_of[14], (D, 2, KV_HEADS * ATT_DIM), D ** -0.5, 0.1875)
    attend_down = noise(streams_of[15], (ATT_HEADS * ATT_DIM, D), 4 ** -0.5, 3.0, ((0, 4),))
    ffn_gain = jnp.clip(1.0 + 0.1 * jax.random.normal(streams_of[16], (D,), jnp.float32), 0.5, 1.5)
    ffn_in = noise(streams_of[17], (D, 2, FF), D ** -0.5, 0.1875, ((2, 4),))
    ffn_down = noise(streams_of[18], (FF, D), FF ** -0.5, 0.125, ((0, 4),))
    return {"tokens": tokens, "cotangent": cotangent, "doc_starts": doc_starts, "norm_gain": norm_gain, "mixer_proj": mixer_proj, "state_proj": state_proj, "step_proj": step_proj, "step_bias": step_bias, "decay_log": decay_log, "skip_gain": skip_gain, "conv_mixer": conv_mixer, "conv_state": conv_state, "mixer_down": mixer_down, "query_proj": query_proj, "keyval_proj": keyval_proj, "attend_down": attend_down, "ffn_gain": ffn_gain, "ffn_in": ffn_in, "ffn_down": ffn_down}


@jax.custom_vjp
def low(v):
    return lax.optimization_barrier(v.astype(jnp.bfloat16)).astype(jnp.float32)

@jax.custom_vjp
def low_back(v):
    return v

def low_keep(v):
    return (low(v), None)

def low_pass(kept, grad):
    return (grad,)

def back_keep(v):
    return (v, None)

def back_low(kept, grad):
    return (low(grad),)
low.defvjp(low_keep, low_pass)
low_back.defvjp(back_keep, back_low)
EPSILON = 1e-05
PRECISE = lax.Precision.HIGHEST
ROPE_BASE = 10000.0

def rms_norm(values, gain_vec):
    return values * lax.rsqrt(lax.optimization_barrier(jnp.mean(values * values, axis=-1, keepdims=True)) + EPSILON) * gain_vec

def silu_value(values):
    return values * jax.nn.sigmoid(values)

def doc_info(starts, length):
    places = jnp.arange(length, dtype=jnp.int32)
    passed = starts[None, :] <= places[:, None]
    doc_ids = lax.optimization_barrier(jnp.sum(passed.astype(jnp.int32), axis=1))
    begins = lax.optimization_barrier(jnp.max(jnp.where(passed, starts[None, :], 0), axis=1))
    return (doc_ids, places - begins)

def rotate(values, positions):
    half_dim = values.shape[-1] // 2
    inv_freq = jnp.exp(jnp.arange(half_dim).astype(jnp.float32) * (-2.0 * math.log(ROPE_BASE) / values.shape[-1]))
    angles = positions.astype(jnp.float32)[:, None] * inv_freq[None, :]
    cosine = jnp.cos(angles)[:, None, :]
    sine_part = jnp.sin(angles)[:, None, :]
    front_half = values[..., :half_dim]
    back_half = values[..., half_dim:]
    return jnp.concatenate([front_half * cosine - back_half * sine_part, back_half * cosine + front_half * sine_part], axis=-1)

def causal_conv(values, conv_weight, positions):
    tap_count = conv_weight.shape[0]
    length = values.shape[0]
    padded = jnp.concatenate([jnp.zeros((tap_count - 1, values.shape[1]), values.dtype), values], axis=0)
    result = jnp.zeros_like(values)
    for tap_index in range(tap_count):
        lag_steps = tap_count - 1 - tap_index
        result = result + jnp.where((positions >= lag_steps)[:, None], padded[tap_index:tap_index + length] * conv_weight[tap_index], 0.0)
    return result

def state_block(state_in, block_inputs):
    inner_act, b_vec, c_vec, step_size, log_keep, doc_ids, positions = block_inputs
    piece_len = inner_act.shape[0]
    local_place = jnp.arange(piece_len, dtype=jnp.int32)
    cum_keep = jnp.cumsum(log_keep, axis=0)
    causal_mask = (local_place[:, None] >= local_place[None, :]) & (doc_ids[:, None] == doc_ids[None, :])
    gap_log = cum_keep[:, None, :] - cum_keep[None, :, :]
    decay_mat = jnp.where(causal_mask[:, :, None], jnp.exp(jnp.where(causal_mask[:, :, None], gap_log, 0.0)), 0.0)
    gram_mat = jnp.dot(c_vec, b_vec.T, precision=PRECISE)
    drive_in = inner_act * step_size[:, :, None]
    state_out = jnp.einsum('tsh,shp->thp', gram_mat[:, :, None] * decay_mat, drive_in, precision=PRECISE)
    lift_rate = jnp.where((positions > local_place)[:, None], jnp.exp(cum_keep), 0.0)
    state_out = state_out + jnp.einsum('tn,hpn->thp', c_vec, state_in, precision=PRECISE) * lift_rate[:, :, None]
    tail_rate = jnp.where((doc_ids == doc_ids[-1])[:, None], jnp.exp(cum_keep[-1][None, :] - cum_keep), 0.0)
    fresh_state = jnp.einsum('sh,shp,sn->hpn', tail_rate, drive_in, b_vec, precision=PRECISE)
    keep_rate = jnp.where(positions[-1] > piece_len - 1, jnp.exp(cum_keep[-1]), 0.0)
    return (keep_rate[:, None, None] * state_in + fresh_state, state_out)

def block_forward(weights, row_in, starts):
    norm_gain, mixer_proj, state_proj, step_proj, step_bias, decay_log, skip_gain, conv_mixer, conv_state, mixer_down, query_proj, keyval_proj, attend_down, ffn_gain, ffn_in, ffn_down = weights
    length = row_in.shape[0]
    doc_ids, positions = doc_info(starts, length)
    normed = low(rms_norm(row_in, norm_gain))
    mixer_pre = low_back(jnp.einsum('td,dkc->tkc', normed, mixer_proj, precision=PRECISE))
    gate_pre = mixer_pre[:, 0]
    inner_in = low(mixer_pre[:, 1])
    state_pre = low(low_back(jnp.dot(normed, state_proj, precision=PRECISE)))
    step_pre = low_back(jnp.dot(normed, step_proj, precision=PRECISE))
    query_pre = low_back(jnp.dot(normed, query_proj, precision=PRECISE))
    keyval_pre = low_back(jnp.einsum('td,dkc->tkc', normed, keyval_proj, precision=PRECISE))
    conv_pre = causal_conv(jnp.concatenate([inner_in, state_pre], axis=1), jnp.concatenate([conv_mixer, conv_state], axis=1), positions)
    activated = low(silu_value(conv_pre))
    inner_width = mixer_proj.shape[2]
    head_count = step_bias.shape[0]
    head_dim = inner_width // head_count
    states = state_proj.shape[1] // 2
    inner_act = activated[:, :inner_width].reshape(length, head_count, head_dim)
    b_vec = activated[:, inner_width:inner_width + states]
    c_vec = activated[:, inner_width + states:]
    step_size = jax.nn.softplus(step_pre + step_bias)
    log_keep = -step_size * jnp.exp(decay_log)
    block_total = length // CH

    def split(values):
        return values.reshape((block_total, CH) + values.shape[1:])
    init_state = jnp.zeros((head_count, head_dim, states), jnp.float32)
    final_state, state_out = lax.scan(jax.checkpoint(state_block), init_state, (split(inner_act), split(b_vec), split(c_vec), split(step_size), split(log_keep), split(doc_ids), split(positions)))
    state_out = state_out.reshape(length, head_count, head_dim) + skip_gain[:, None] * inner_act
    gated = low((state_out * silu_value(gate_pre.reshape(length, head_count, head_dim))).reshape(length, inner_width))
    mixer_part = jnp.dot(gated, mixer_down, precision=PRECISE)
    query_heads = query_proj.shape[1] // ATT_DIM
    kv_heads = keyval_proj.shape[2] // ATT_DIM
    query_rot = low(rotate(query_pre.reshape(length, query_heads, ATT_DIM), positions))
    key_rot = low(rotate(keyval_pre[:, 0].reshape(length, kv_heads, ATT_DIM), positions))
    value_low = low(keyval_pre[:, 1].reshape(length, kv_heads, ATT_DIM))
    key_rot = jnp.repeat(key_rot, query_heads // kv_heads, axis=1)
    value_low = jnp.repeat(value_low, query_heads // kv_heads, axis=1)
    places = jnp.arange(length, dtype=jnp.int32)

    def attend(first_place):
        query_block = lax.dynamic_slice_in_dim(query_rot, first_place, CH, 0)
        query_places = first_place + jnp.arange(CH, dtype=jnp.int32)
        query_docs = lax.dynamic_slice_in_dim(doc_ids, first_place, CH, 0)
        scores = low_back(jnp.einsum('thd,shd->hts', query_block, key_rot, precision=PRECISE) * ATT_DIM ** (-0.5))
        allowed = (places[None, :] <= query_places[:, None]) & (doc_ids[None, :] == query_docs[:, None])
        scores = jnp.where(allowed[None], scores, -1e+30)
        row_top = lax.optimization_barrier(jnp.max(scores, axis=-1, keepdims=True))
        expo = jnp.exp(scores - row_top)
        soft_probs = expo / lax.optimization_barrier(jnp.sum(expo, axis=-1, keepdims=True))
        return jnp.einsum('hts,shd->thd', low(soft_probs), value_low, precision=PRECISE)
    firsts = jnp.arange(length // CH, dtype=jnp.int32) * CH
    attended = lax.map(jax.checkpoint(attend), firsts).reshape(length, query_heads * ATT_DIM)
    attended = low_back(low(attended))
    attend_part = jnp.dot(attended, attend_down, precision=PRECISE)
    mixed_sum = low_back(mixer_part + attend_part)
    middle = row_in + mixed_sum
    middle_low = low(rms_norm(middle, ffn_gain))
    ffn_pre = low_back(jnp.einsum('td,dkf->tkf', middle_low, ffn_in, precision=PRECISE))
    hidden = low(silu_value(ffn_pre[:, 0]) * ffn_pre[:, 1])
    ffn_part = low_back(jnp.dot(hidden, ffn_down, precision=PRECISE))
    return middle + ffn_part

def reference(tokens, cotangent, doc_starts, norm_gain, mixer_proj, state_proj, step_proj, step_bias, decay_log, skip_gain, conv_mixer, conv_state, mixer_down, query_proj, keyval_proj, attend_down, ffn_gain, ffn_in, ffn_down):
    weights = tuple((value.astype(jnp.float32) for value in (norm_gain, mixer_proj, state_proj, step_proj, step_bias, decay_log, skip_gain, conv_mixer, conv_state, mixer_down, query_proj, keyval_proj, attend_down, ffn_gain, ffn_in, ffn_down)))

    def row_step(grad_total, row_inputs):
        row_in, row_grad, starts = row_inputs
        row_out, backward = jax.vjp(lambda params, values: block_forward(params, values, starts), weights, row_in.astype(jnp.float32))
        weight_grads, input_grad = backward(row_grad.astype(jnp.float32))
        grad_total = jax.tree.map(lambda first_val, second_val: first_val + second_val, grad_total, weight_grads)
        return (grad_total, (row_out.astype(jnp.bfloat16), input_grad.astype(jnp.bfloat16)))
    zero_grads = jax.tree.map(jnp.zeros_like, weights)
    grads, (output, token_grad) = lax.scan(row_step, zero_grads, (tokens, cotangent, doc_starts))
    return (output, token_grad, grads[0], grads[1], grads[2], grads[3], grads[4], grads[5], grads[6], grads[7], grads[8], grads[9], grads[10], grads[11], grads[12], grads[13], grads[14], grads[15])
```

```python
from functools import partial
import math

import jax
import jax.numpy as jnp
from jax import lax
from jax.experimental import pallas as pl
from jax.experimental.pallas import tpu as pltpu
from jax.sharding import PartitionSpec as P

ATT_HEADS = 8
KV_HEADS = 2
ATT_DIM = 64


EPSILON = 1e-05
PRECISE = lax.Precision.DEFAULT
ROPE_BASE = 10000.0
FLOOR_SCORE = -1e30
FIRST_TOP = -1e29


def shifted(block, axis, distance):
    devices = range(lax.axis_size(axis))
    route = [(i - distance, i) for i in devices if i - distance in devices]
    return lax.ppermute(block, axis, route)


def carried_in(keeps, states, index, reverse):
    size = keeps.shape[0]
    order = jnp.arange(size)
    source, between = order[:, None], order[None, :]
    if reverse:
        inside = (between < source) & (between > index)
        reached = order > index
    else:
        inside = (between > source) & (between < index)
        reached = order < index
    weight = jnp.prod(
        jnp.where(inside[:, :, None, None], keeps.astype(jnp.float32)[None], 1.0), axis=1
    )
    weight = jnp.where(reached[:, None, None], weight, 0.0)
    return jnp.sum(weight[..., None, None] * states.astype(jnp.float32), axis=0)


def running_sum(values):
    length = values.shape[1]
    steps = jnp.arange(length)
    lower = (steps[:, None] >= steps[None, :]).astype(jnp.float32)
    return jnp.einsum("ts,rsh->rth", lower, values, precision=lax.Precision.HIGHEST)


def silu_value(values):
    return values * jax.nn.sigmoid(values)


def silu_slope(values):
    logistic = jax.nn.sigmoid(values)
    return logistic * (1.0 + values * (1.0 - logistic))


def doc_layout(starts, offset, length):
    places = offset + jnp.arange(length, dtype=jnp.int32)
    passed = starts[:, None, :] <= places[None, :, None]
    doc_ids = jnp.sum(passed.astype(jnp.int32), axis=2)
    begins = jnp.max(jnp.where(passed, starts[:, None, :], 0), axis=2)
    return (doc_ids, places[None, :] - begins)


def rotate(values, positions, signed):
    half_dim = values.shape[-1] // 2
    inv_freq = jnp.exp(
        jnp.arange(half_dim).astype(jnp.float32) * (-2.0 * math.log(ROPE_BASE) / values.shape[-1])
    )
    angles = positions.astype(jnp.float32)[:, :, None] * inv_freq
    cosine = jnp.cos(angles)[:, :, None, :]
    sine_part = signed * jnp.sin(angles)[:, :, None, :]
    front_half = values[..., :half_dim]
    back_half = values[..., half_dim:]
    return jnp.concatenate(
        [front_half * cosine - back_half * sine_part, back_half * cosine + front_half * sine_part],
        axis=-1,
    )


def norm_forward(values, gain_vec):
    scaled = lax.rsqrt(jnp.mean(values * values, axis=-1, keepdims=True) + EPSILON)
    normed = values * scaled
    return (normed, scaled, normed * gain_vec)


def norm_backward(upstream, normed, scaled, gain_vec):
    inner_grad = upstream * gain_vec
    back_grad = scaled * (
        inner_grad - normed * jnp.mean(inner_grad * normed, axis=-1, keepdims=True)
    )
    return (back_grad, jnp.sum(upstream * normed, axis=(0, 1)))


def state_summary(doc_ids, positions, inner_act, b_vec, step_size, log_keep):
    piece_len = inner_act.shape[1]
    cum_keep = running_sum(log_keep)
    drive_in = inner_act * step_size[..., None]
    tail_rate = jnp.where(
        (doc_ids == doc_ids[:, -1:])[:, :, None], jnp.exp(cum_keep[:, -1:, :] - cum_keep), 0.0
    )
    fresh_state = jnp.einsum("rsh,rshp,rsn->rhpn", tail_rate, drive_in, b_vec, precision=PRECISE)
    keep_rate = jnp.where(positions[:, -1:] > piece_len - 1, jnp.exp(cum_keep[:, -1]), 0.0)
    return (fresh_state, keep_rate)


def state_output(doc_ids, positions, inner_act, b_vec, c_vec, step_size, log_keep, entering):
    piece_len = inner_act.shape[1]
    local_place = jnp.arange(piece_len, dtype=jnp.int32)
    cum_keep = running_sum(log_keep)
    causal_mask = (local_place[:, None] >= local_place[None, :])[None] & (
        doc_ids[:, :, None] == doc_ids[:, None, :]
    )
    gap_log = cum_keep[:, :, None, :] - cum_keep[:, None, :, :]
    decay_mat = jnp.where(
        causal_mask[..., None], jnp.exp(jnp.where(causal_mask[..., None], gap_log, 0.0)), 0.0
    )
    gram_mat = jnp.einsum("rtn,rsn->rts", c_vec, b_vec, precision=PRECISE)
    drive_in = inner_act * step_size[..., None]
    state_out = jnp.einsum(
        "rtsh,rshp->rthp", gram_mat[..., None] * decay_mat, drive_in, precision=PRECISE
    )
    lift_rate = jnp.where((positions > local_place)[:, :, None], jnp.exp(cum_keep), 0.0)
    return (
        state_out
        + jnp.einsum("rtn,rhpn->rthp", c_vec, entering, precision=PRECISE) * lift_rate[..., None]
    )


def inner_dot(left, right):
    return lax.dot_general(left, right, (((1,), (1,)), ((), ())), preferred_element_type=jnp.float32)


def attend_kernel(span, low_ref, high_ref, query_ref, place_ref, begin_ref, kv_ref, kvt_ref, out_ref, stat_ref):
    row = pl.program_id(0)
    dim = query_ref.shape[2]
    width = query_ref.shape[1]
    query = query_ref[0]
    place = place_ref[0]
    begin = begin_ref[0]

    def step(block, carry):
        top, total, acc = carry
        at = pl.multiple_of(block * span, span)
        key = kv_ref[0, pl.ds(at, span), :dim]
        value_t = kvt_ref[0, dim:, pl.ds(at, span)]
        scores = inner_dot(key, query)
        key_place = at + lax.broadcasted_iota(jnp.int32, scores.shape, 0)
        allowed = (key_place <= place) & (key_place >= begin)
        scores = jnp.where(allowed, scores, FLOOR_SCORE)
        new_top = jnp.maximum(top, jnp.max(scores, axis=0, keepdims=True))
        probs = jnp.exp(scores - new_top)
        scale = jnp.exp(top - new_top)
        total = total * scale + jnp.sum(probs, axis=0, keepdims=True)
        acc = acc * scale + jnp.dot(
            value_t, probs.astype(jnp.bfloat16), preferred_element_type=jnp.float32
        )
        return new_top, total, acc

    top, total, acc = lax.fori_loop(
        low_ref[row],
        high_ref[row],
        step,
        (
            jnp.full((1, width), FIRST_TOP, jnp.float32),
            jnp.zeros((1, width), jnp.float32),
            jnp.zeros((dim, width), jnp.float32),
        ),
    )
    out_ref[0] = acc / total
    stat_ref[0] = top + jnp.log(total)


def attend_back_kernel(
    span, low_ref, high_ref, query_ref, grad_ref, place_ref, begin_ref, stat_ref, dot_ref, kv_ref, kvt_ref,
    query_grad_ref, kv_grad_ref,
):
    row = pl.program_id(0)
    dim = query_ref.shape[2]
    width = query_ref.shape[1]
    query = query_ref[0]
    grad = grad_ref[0]
    place = place_ref[0]
    begin = begin_ref[0]
    stat = stat_ref[0]
    dots = dot_ref[0]
    kv_grad_ref[...] = jnp.zeros_like(kv_grad_ref)

    def step(block, query_grad):
        at = pl.multiple_of(block * span, span)
        key = kv_ref[0, pl.ds(at, span), :dim]
        value = kv_ref[0, pl.ds(at, span), dim:]
        key_t = kvt_ref[0, :dim, pl.ds(at, span)]
        scores = inner_dot(key, query)
        key_place = at + lax.broadcasted_iota(jnp.int32, scores.shape, 0)
        allowed = (key_place <= place) & (key_place >= begin)
        probs = jnp.exp(jnp.where(allowed, scores - stat, FLOOR_SCORE))
        prob_grad = inner_dot(value, grad)
        score_grad = (probs * (prob_grad - dots)).astype(jnp.bfloat16)
        value_grad = jnp.dot(probs.astype(jnp.bfloat16), grad, preferred_element_type=jnp.float32)
        key_grad = jnp.dot(score_grad, query, preferred_element_type=jnp.float32)
        kv_grad_ref[0, pl.ds(at, span), :] = jnp.concatenate(
            [key_grad, value_grad], axis=1
        ).astype(jnp.bfloat16)
        return query_grad + jnp.dot(key_t, score_grad, preferred_element_type=jnp.float32)

    query_grad_ref[0] = lax.fori_loop(
        low_ref[row], high_ref[row], step, jnp.zeros((dim, width), jnp.float32)
    )


def row_spec(*shape):
    return pl.BlockSpec((1,) + shape, lambda r, *_: (r,) + (0,) * len(shape))


def attend_forward(span, low, high, query, place, begin, keyval, keyval_t):
    rows, width, dim = query.shape
    full = keyval.shape[1]
    return pl.pallas_call(
        partial(attend_kernel, span),
        grid_spec=pltpu.PrefetchScalarGridSpec(
            num_scalar_prefetch=2,
            grid=(rows,),
            in_specs=[
                row_spec(width, dim), row_spec(1, width), row_spec(1, width),
                row_spec(full, 2 * dim), row_spec(2 * dim, full),
            ],
            out_specs=[row_spec(dim, width), row_spec(1, width)],
        ),
        out_shape=[
            jax.ShapeDtypeStruct((rows, dim, width), jnp.float32),
            jax.ShapeDtypeStruct((rows, 1, width), jnp.float32),
        ],
        compiler_params=pltpu.CompilerParams(vmem_limit_bytes=48 * 1024 * 1024),
    )(low, high, query, place, begin, keyval, keyval_t)


def attend_backward(span, low, high, query, grad, place, begin, stat, dots, keyval, keyval_t):
    rows, width, dim = query.shape
    full = keyval.shape[1]
    return pl.pallas_call(
        partial(attend_back_kernel, span),
        grid_spec=pltpu.PrefetchScalarGridSpec(
            num_scalar_prefetch=2,
            grid=(rows,),
            in_specs=[
                row_spec(width, dim), row_spec(width, dim), row_spec(1, width), row_spec(1, width),
                row_spec(1, width), row_spec(1, width),
                row_spec(full, 2 * dim), row_spec(2 * dim, full),
            ],
            out_specs=[row_spec(dim, width), row_spec(full, 2 * dim)],
        ),
        out_shape=[
            jax.ShapeDtypeStruct((rows, dim, width), jnp.float32),
            jax.ShapeDtypeStruct((rows, full, 2 * dim), jnp.bfloat16),
        ],
        compiler_params=pltpu.CompilerParams(vmem_limit_bytes=48 * 1024 * 1024),
    )(low, high, query, grad, place, begin, stat, dots, keyval, keyval_t)


def local(
    tokens,
    cotangent,
    doc_starts,
    norm_gain,
    mixer_proj,
    state_proj,
    step_proj,
    step_bias,
    decay_log,
    skip_gain,
    conv_mixer,
    conv_state,
    mixer_down,
    query_proj,
    keyval_proj,
    attend_down,
    ffn_gain,
    ffn_in,
    ffn_down,
):
    row_count, length, model_width = tokens.shape
    offset = lax.axis_index("seq") * length
    head_ways = lax.axis_size("head")
    share_len = length // head_ways
    share_start = lax.axis_index("head") * share_len
    inner_width = mixer_proj.shape[2]
    head_count = step_bias.shape[0]
    head_dim = inner_width // head_count
    states = state_proj.shape[1] // 2
    tap_count = conv_mixer.shape[0]
    local_heads = query_proj.shape[1] // ATT_DIM
    kv_total = keyval_proj.shape[2] // ATT_DIM
    group_size = ATT_HEADS // KV_HEADS
    kv_index = lax.axis_index("head") * local_heads // group_size
    score_scale = ATT_DIM ** (-0.5)
    doc_ids, positions = doc_layout(doc_starts, offset, length)
    places = jnp.arange(length, dtype=jnp.int32)

    def share_of(values):
        return lax.dynamic_slice_in_dim(values, share_start, share_len, 1)

    inputs = tokens.astype(jnp.float32)
    normed_one, scaled_one, gained_one = norm_forward(inputs, norm_gain)
    normed_low = gained_one.astype(jnp.bfloat16)
    mixer_pre = jnp.einsum(
        "rtd,dkc->rtkc", normed_low, mixer_proj, preferred_element_type=jnp.float32
    )
    gate_view = mixer_pre[:, :, 0].reshape(row_count, length, head_count, head_dim)
    state_pre = jnp.einsum(
        "rtd,dc->rtc", normed_low, state_proj, preferred_element_type=jnp.float32
    )
    step_pre = jnp.einsum("rtd,dh->rth", normed_low, step_proj, preferred_element_type=jnp.float32)
    query_pre = jnp.einsum(
        "rtd,dc->rtc", normed_low, query_proj, preferred_element_type=jnp.float32
    )
    keyval_mine = lax.dynamic_slice_in_dim(keyval_proj, kv_index * ATT_DIM, ATT_DIM, 2)
    keyval_pre = jnp.einsum(
        "rtd,dkc->rtkc", normed_low, keyval_mine, preferred_element_type=jnp.float32
    )
    conv_input = jnp.concatenate([mixer_pre[:, :, 1], state_pre], axis=2).astype(jnp.bfloat16)
    conv_weight = jnp.concatenate([conv_mixer, conv_state], axis=1)
    before = shifted(conv_input[:, length - (tap_count - 1) :], "seq", 1)
    padded = jnp.concatenate([before, conv_input], axis=1)
    conv_pre = jnp.zeros(conv_input.shape, jnp.float32)
    for tap_index in range(tap_count):
        lag_steps = tap_count - 1 - tap_index
        conv_pre = conv_pre + jnp.where(
            (positions >= lag_steps)[:, :, None],
            padded[:, tap_index : tap_index + length] * conv_weight[tap_index],
            0.0,
        )
    activated = silu_value(conv_pre).astype(jnp.bfloat16)
    mixer_act = (
        activated[:, :, :inner_width]
        .reshape(row_count, length, head_count, head_dim)
        .astype(jnp.float32)
    )
    state_b = activated[:, :, inner_width : inner_width + states].astype(jnp.float32)
    state_c = activated[:, :, inner_width + states :].astype(jnp.float32)
    step_size = jax.nn.softplus(step_pre + step_bias)
    decay_rates = jnp.exp(decay_log)
    log_keep = -step_size * decay_rates
    (fresh_state, keep_rate), summary_back = jax.vjp(
        partial(state_summary, doc_ids, positions), mixer_act, state_b, step_size, log_keep
    )
    seq_index = lax.axis_index("seq")
    all_keep = lax.all_gather(keep_rate.astype(jnp.bfloat16), "seq")
    entering = carried_in(
        all_keep, lax.all_gather(fresh_state.astype(jnp.bfloat16), "seq"), seq_index, False
    )
    mixed_state, output_back = jax.vjp(
        partial(state_output, doc_ids, positions),
        mixer_act,
        state_b,
        state_c,
        step_size,
        log_keep,
        entering,
    )
    full_state = mixed_state + skip_gain[:, None] * mixer_act
    gated_low = (
        (full_state * silu_value(gate_view))
        .reshape(row_count, length, inner_width)
        .astype(jnp.bfloat16)
    )
    mixer_part = jnp.einsum(
        "rtc,cd->rtd", gated_low, mixer_down, preferred_element_type=jnp.float32
    )
    query_rot = rotate(
        query_pre.reshape(row_count, length, local_heads, ATT_DIM), positions, 1.0
    ).astype(jnp.bfloat16)
    key_rot = rotate(keyval_pre[:, :, 0][:, :, None], positions, 1.0)[:, :, 0].astype(jnp.bfloat16)
    value_low = keyval_pre[:, :, 1].astype(jnp.bfloat16)
    keyval_all = lax.all_gather(
        jnp.concatenate([key_rot, value_low], axis=2), "seq", axis=1, tiled=True
    )
    keyval_t = jnp.swapaxes(keyval_all, 1, 2)
    query_scaled = (
        jnp.swapaxes(query_rot, 1, 2).reshape(row_count, local_heads * length, ATT_DIM)
        * jnp.bfloat16(score_scale)
    )
    begins = offset + places[None, :] - positions
    place_row = jnp.tile(offset + places, local_heads)[None, None, :]
    place_row = jnp.broadcast_to(place_row, (row_count, 1, local_heads * length))
    begin_row = jnp.tile(begins, (1, local_heads))[:, None, :]
    low_block = begins[:, 0] // length
    high_block = jnp.broadcast_to(lax.axis_index("seq") + 1, (row_count,)).astype(jnp.int32)
    attended_t, stat_row = attend_forward(
        length, low_block, high_block, query_scaled, place_row, begin_row, keyval_all, keyval_t
    )
    attended = attended_t.reshape(row_count, ATT_DIM, local_heads, length).transpose(0, 3, 2, 1)
    attended_low = attended.astype(jnp.bfloat16).reshape(row_count, length, local_heads * ATT_DIM)
    attend_part = jnp.einsum(
        "rtc,cd->rtd", attended_low, attend_down, preferred_element_type=jnp.float32
    )
    mixed_sum = lax.psum((mixer_part + attend_part).astype(jnp.bfloat16), "head").astype(
        jnp.float32
    )
    middle = inputs + mixed_sum
    normed_two, scaled_two, gained_two = norm_forward(middle, ffn_gain)
    middle_low = gained_two.astype(jnp.bfloat16)
    ffn_pre = jnp.einsum("rtd,dkf->rtkf", middle_low, ffn_in, preferred_element_type=jnp.float32)
    hidden = (silu_value(ffn_pre[:, :, 0]) * ffn_pre[:, :, 1]).astype(jnp.bfloat16)
    ffn_part = jnp.einsum("rtf,fd->rtd", hidden, ffn_down, preferred_element_type=jnp.float32)
    ffn_share_sum = lax.psum_scatter(
        ffn_part.astype(jnp.bfloat16), "head", scatter_dimension=1, tiled=True
    ).astype(jnp.float32)
    output_share = (share_of(middle) + ffn_share_sum).astype(jnp.bfloat16)
    hidden_grad = jnp.einsum("rtd,fd->rtf", cotangent, ffn_down, preferred_element_type=jnp.float32)
    ffn_down_grad = jnp.einsum("rtf,rtd->fd", hidden, cotangent, preferred_element_type=jnp.float32)
    gate_value = ffn_pre[:, :, 0]
    ffn_pre_grad = jnp.stack(
        [
            hidden_grad * ffn_pre[:, :, 1] * silu_slope(gate_value),
            hidden_grad * silu_value(gate_value),
        ],
        axis=2,
    ).astype(jnp.bfloat16)
    ffn_in_grad = jnp.einsum(
        "rtd,rtkf->dkf", middle_low, ffn_pre_grad, preferred_element_type=jnp.float32
    )
    middle_low_part = jnp.einsum(
        "rtkf,dkf->rtd", ffn_pre_grad, ffn_in, preferred_element_type=jnp.float32
    )
    low_grad_share = lax.psum_scatter(
        middle_low_part.astype(jnp.bfloat16), "head", scatter_dimension=1, tiled=True
    ).astype(jnp.float32)
    norm_back_share, ffn_gain_part = norm_backward(
        low_grad_share, share_of(normed_two), share_of(scaled_two), ffn_gain
    )
    middle_grad_share = share_of(cotangent).astype(jnp.float32) + norm_back_share
    mixed_low = lax.all_gather(middle_grad_share.astype(jnp.bfloat16), "head", axis=1, tiled=True)
    gated_grad = jnp.einsum(
        "rtd,cd->rtc", mixed_low, mixer_down, preferred_element_type=jnp.float32
    ).reshape(row_count, length, head_count, head_dim)
    mixer_down_grad = jnp.einsum(
        "rtc,rtd->cd", gated_low, mixed_low, preferred_element_type=jnp.float32
    )
    attended_grad = jnp.einsum(
        "rtd,cd->rtc", mixed_low, attend_down, preferred_element_type=jnp.float32
    ).astype(jnp.bfloat16)
    attend_down_grad = jnp.einsum(
        "rtc,rtd->cd", attended_low, mixed_low, preferred_element_type=jnp.float32
    )
    attended_grad = attended_grad.reshape(row_count, length, local_heads, ATT_DIM)
    grad_dot = jnp.swapaxes(jnp.sum(attended_grad.astype(jnp.float32) * attended, axis=-1), 1, 2)

    query_grad_t, keyval_grads = attend_backward(
        length,
        low_block,
        high_block,
        query_scaled,
        jnp.swapaxes(attended_grad, 1, 2).reshape(row_count, local_heads * length, ATT_DIM),
        place_row,
        begin_row,
        stat_row,
        grad_dot.reshape(row_count, 1, local_heads * length),
        keyval_all,
        keyval_t,
    )
    query_grad = (
        query_grad_t.reshape(row_count, ATT_DIM, local_heads, length).transpose(0, 3, 2, 1)
        * score_scale
    )
    keyval_grad = lax.psum_scatter(
        keyval_grads, "seq", scatter_dimension=1, tiled=True
    ).astype(jnp.float32)
    key_grad, value_grad = keyval_grad[..., :ATT_DIM], keyval_grad[..., ATT_DIM:]
    query_low = (
        rotate(query_grad, positions, -1.0)
        .reshape(row_count, length, local_heads * ATT_DIM)
        .astype(jnp.bfloat16)
    )
    keyval_own = jnp.stack(
        [rotate(key_grad[:, :, None], positions, -1.0)[:, :, 0], value_grad], axis=2
    )
    keyval_part = jnp.zeros((row_count, length, 2, kv_total, ATT_DIM), jnp.float32)
    keyval_part = lax.dynamic_update_slice_in_dim(
        keyval_part, keyval_own[:, :, :, None], kv_index, 3
    )
    state_grad = gated_grad * silu_value(gate_view)
    gate_grad = gated_grad * full_state * silu_slope(gate_view)
    skip_gain_grad = jnp.sum(state_grad * mixer_act, axis=(0, 1, 3))
    lift_rate = jnp.where(
        (positions > places)[:, :, None], jnp.exp(running_sum(log_keep)), 0.0
    )
    local_grad = jnp.einsum(
        "rthp,rtn->rhpn", state_grad * lift_rate[..., None], state_c, precision=PRECISE
    )
    after_grad = carried_in(
        all_keep, lax.all_gather(local_grad.astype(jnp.bfloat16), "seq"), seq_index, True
    )
    keep_grad = jnp.sum(after_grad * entering, axis=(2, 3))
    act_grad_one, b_grad_one, step_grad_one, log_grad_one = summary_back((after_grad, keep_grad))
    act_grad_two, b_grad_two, c_grad, step_grad_two, log_grad_two, entering_grad = output_back(
        state_grad
    )
    mixer_act_grad = act_grad_one + act_grad_two + state_grad * skip_gain[:, None]
    log_grad = log_grad_one + log_grad_two
    step_grad = step_grad_one + step_grad_two - log_grad * decay_rates
    decay_log_grad = jnp.sum(log_grad * log_keep, axis=(0, 1))
    step_pre_grad = step_grad * jax.nn.sigmoid(step_pre + step_bias)
    step_bias_grad = jnp.sum(step_pre_grad, axis=(0, 1))
    step_low = step_pre_grad.astype(jnp.bfloat16)
    act_grad = jnp.concatenate(
        [mixer_act_grad.reshape(row_count, length, inner_width), b_grad_one + b_grad_two, c_grad],
        axis=2,
    )
    pre_grad = act_grad * silu_slope(conv_pre)
    state_total, keyval_total = (
        lax.psum(pre_grad[:, :, inner_width:].astype(jnp.bfloat16), "head").astype(jnp.float32),
        lax.psum(keyval_part.astype(jnp.bfloat16), "head").astype(jnp.float32),
    )
    pre_grad = jnp.concatenate([pre_grad[:, :, :inner_width], state_total], axis=2)
    padded_grad = jnp.zeros((row_count, length + tap_count - 1, pre_grad.shape[2]), jnp.float32)
    conv_grads = []
    for tap_index in range(tap_count):
        lag_steps = tap_count - 1 - tap_index
        masked = jnp.where((positions >= lag_steps)[:, :, None], pre_grad, 0.0)
        conv_grads.append(jnp.sum(masked * padded[:, tap_index : tap_index + length], axis=(0, 1)))
        padded_grad = padded_grad + jnp.pad(
            masked * conv_weight[tap_index], ((0, 0), (tap_index, lag_steps), (0, 0))
        )
    conv_weight_grad = jnp.stack(conv_grads, axis=0)
    rim_grad = shifted(padded_grad[:, : tap_count - 1], "seq", -1)
    conv_input_grad = padded_grad[:, tap_count - 1 :] + jnp.pad(
        rim_grad, ((0, 0), (length - (tap_count - 1), 0), (0, 0))
    )
    mixer_low = jnp.stack(
        [gate_grad.reshape(row_count, length, inner_width), conv_input_grad[:, :, :inner_width]],
        axis=2,
    ).astype(jnp.bfloat16)
    state_low = conv_input_grad[:, :, inner_width:].astype(jnp.bfloat16)
    keyval_low = keyval_total.reshape(row_count, length, 2, kv_total * ATT_DIM).astype(jnp.bfloat16)
    mixer_proj_grad = jnp.einsum(
        "rtd,rtkc->dkc", normed_low, mixer_low, preferred_element_type=jnp.float32
    )
    state_proj_grad = jnp.einsum(
        "rtd,rtc->dc", normed_low, state_low, preferred_element_type=jnp.float32
    )
    step_proj_grad = jnp.einsum(
        "rtd,rth->dh", normed_low, step_low, preferred_element_type=jnp.float32
    )
    query_proj_grad = jnp.einsum(
        "rtd,rtc->dc", normed_low, query_low, preferred_element_type=jnp.float32
    )
    keyval_proj_grad = jnp.einsum(
        "rtd,rtkc->dkc", normed_low, keyval_low, preferred_element_type=jnp.float32
    )
    head_part = (
        jnp.einsum("rtkc,dkc->rtd", mixer_low, mixer_proj, preferred_element_type=jnp.float32)
        + jnp.einsum("rth,dh->rtd", step_low, step_proj, preferred_element_type=jnp.float32)
        + jnp.einsum("rtc,dc->rtd", query_low, query_proj, preferred_element_type=jnp.float32)
    )
    common_share = jnp.einsum(
        "rtc,dc->rtd", share_of(state_low), state_proj, preferred_element_type=jnp.float32
    ) + jnp.einsum(
        "rtkc,dkc->rtd", share_of(keyval_low), keyval_proj, preferred_element_type=jnp.float32
    )
    normed_share = share_of(normed_one)
    norm_rider = jnp.sum(head_part * normed_one, axis=(0, 1)) + jnp.sum(
        common_share * normed_share, axis=(0, 1)
    )
    head_share, ffn_gain_total, norm_gain_total = (
        lax.psum_scatter(
            head_part.astype(jnp.bfloat16), "head", scatter_dimension=1, tiled=True
        ).astype(jnp.float32),
        lax.psum_scatter(
            jnp.broadcast_to(ffn_gain_part[None, None, :], (1, head_ways, model_width)).astype(
                jnp.bfloat16
            ),
            "head",
            scatter_dimension=1,
            tiled=True,
        ).astype(jnp.float32),
        lax.psum_scatter(
            jnp.broadcast_to(norm_rider[None, None, :], (1, head_ways, model_width)).astype(
                jnp.bfloat16
            ),
            "head",
            scatter_dimension=1,
            tiled=True,
        ).astype(jnp.float32),
    )
    ffn_gain_grad = ffn_gain_total.reshape(model_width)
    norm_gain_grad = norm_gain_total.reshape(model_width)
    norm_back_share_one, unused_gain = norm_backward(
        head_share + common_share, normed_share, share_of(scaled_one), norm_gain
    )
    token_share = (middle_grad_share + norm_back_share_one).astype(jnp.bfloat16)
    output, token_grad = (
        lax.all_gather(output_share, "head", axis=1, tiled=True),
        lax.all_gather(token_share, "head", axis=1, tiled=True),
    )
    (
        norm_gain_sum,
        mixer_proj_sum,
        state_proj_sum,
        step_proj_sum,
        step_bias_sum,
        decay_log_sum,
        skip_gain_sum,
        conv_mixer_sum,
        conv_state_sum,
        mixer_down_sum,
        query_proj_sum,
        keyval_proj_sum,
        attend_down_sum,
        ffn_gain_sum,
        ffn_in_sum,
        ffn_down_sum,
    ) = (
        lax.psum(norm_gain_grad.astype(jnp.bfloat16), "seq").astype(jnp.float32),
        lax.psum(mixer_proj_grad.astype(jnp.bfloat16), "seq").astype(jnp.float32),
        lax.psum(state_proj_grad.astype(jnp.bfloat16), "seq").astype(jnp.float32),
        lax.psum(step_proj_grad.astype(jnp.bfloat16), "seq").astype(jnp.float32),
        lax.psum(step_bias_grad.astype(jnp.bfloat16), "seq").astype(jnp.float32),
        lax.psum(decay_log_grad.astype(jnp.bfloat16), "seq").astype(jnp.float32),
        lax.psum(skip_gain_grad.astype(jnp.bfloat16), "seq").astype(jnp.float32),
        lax.psum(conv_weight_grad[:, :inner_width].astype(jnp.bfloat16), "seq").astype(jnp.float32),
        lax.psum(conv_weight_grad[:, inner_width:].astype(jnp.bfloat16), "seq").astype(jnp.float32),
        lax.psum(mixer_down_grad.astype(jnp.bfloat16), "seq").astype(jnp.float32),
        lax.psum(query_proj_grad.astype(jnp.bfloat16), "seq").astype(jnp.float32),
        lax.psum(keyval_proj_grad.astype(jnp.bfloat16), "seq").astype(jnp.float32),
        lax.psum(attend_down_grad.astype(jnp.bfloat16), "seq").astype(jnp.float32),
        lax.psum(ffn_gain_grad.astype(jnp.bfloat16), "seq").astype(jnp.float32),
        lax.psum(ffn_in_grad.astype(jnp.bfloat16), "seq").astype(jnp.float32),
        lax.psum(ffn_down_grad.astype(jnp.bfloat16), "seq").astype(jnp.float32),
    )
    return (
        output,
        token_grad,
        norm_gain_sum,
        mixer_proj_sum,
        state_proj_sum,
        step_proj_sum,
        step_bias_sum,
        decay_log_sum,
        skip_gain_sum,
        conv_mixer_sum,
        conv_state_sum,
        mixer_down_sum,
        query_proj_sum,
        keyval_proj_sum,
        attend_down_sum,
        ffn_gain_sum,
        ffn_in_sum,
        ffn_down_sum,
    )


def solution(mesh):
    placed = (
        P(None, "seq", None),
        P(None, "seq", None),
        P(),
        P(),
        P(None, None, "head"),
        P(),
        P(None, "head"),
        P("head"),
        P("head"),
        P("head"),
        P(None, "head"),
        P(),
        P("head", None),
        P(None, "head"),
        P(),
        P("head", None),
        P(),
        P(None, None, "head"),
        P("head", None),
    )
    return jax.shard_map(
        local,
        mesh=mesh,
        in_specs=placed,
        out_specs=(
            P(None, "seq", None),
            P(None, "seq", None),
            P(),
            P(None, None, "head"),
            P(),
            P(None, "head"),
            P("head"),
            P("head"),
            P("head"),
            P(None, "head"),
            P(),
            P("head", None),
            P(None, "head"),
            P(),
            P("head", None),
            P(),
            P(None, None, "head"),
            P("head", None),
        ),
        check_vma=False,
    )
```

```python
from functools import partial
import math

import jax
import jax.numpy as jnp
from jax import lax
from jax.experimental import pallas as pl
from jax.experimental.pallas import tpu as pltpu
from jax.sharding import PartitionSpec as P

ATT_HEADS = 8
KV_HEADS = 2
ATT_DIM = 64


EPSILON = 1e-05
PRECISE = lax.Precision.DEFAULT
ROPE_BASE = 10000.0
FLOOR_SCORE = -1e30
FIRST_TOP = -1e29


def shifted(block, axis, distance):
    devices = range(lax.axis_size(axis))
    route = [(i - distance, i) for i in devices if i - distance in devices]
    return lax.ppermute(block, axis, route)


def carried_in(keeps, states, index, reverse):
    size = keeps.shape[0]
    order = jnp.arange(size)
    source, between = order[:, None], order[None, :]
    if reverse:
        inside = (between < source) & (between > index)
        reached = order > index
    else:
        inside = (between > source) & (between < index)
        reached = order < index
    weight = jnp.prod(
        jnp.where(inside[:, :, None, None], keeps.astype(jnp.float32)[None], 1.0), axis=1
    )
    weight = jnp.where(reached[:, None, None], weight, 0.0)
    return jnp.sum(weight[..., None, None] * states.astype(jnp.float32), axis=0)


def running_sum(values):
    length = values.shape[1]
    steps = jnp.arange(length)
    lower = (steps[:, None] >= steps[None, :]).astype(jnp.float32)
    return jnp.einsum("ts,rsh->rth", lower, values, precision=lax.Precision.HIGHEST)


def silu_value(values):
    return values * jax.nn.sigmoid(values)


def silu_slope(values):
    logistic = jax.nn.sigmoid(values)
    return logistic * (1.0 + values * (1.0 - logistic))


def doc_layout(starts, offset, length):
    places = offset + jnp.arange(length, dtype=jnp.int32)
    passed = starts[:, None, :] <= places[None, :, None]
    doc_ids = jnp.sum(passed.astype(jnp.int32), axis=2)
    begins = jnp.max(jnp.where(passed, starts[:, None, :], 0), axis=2)
    return (doc_ids, places[None, :] - begins)


def rotate(values, positions, signed):
    half_dim = values.shape[-1] // 2
    inv_freq = jnp.exp(
        jnp.arange(half_dim).astype(jnp.float32) * (-2.0 * math.log(ROPE_BASE) / values.shape[-1])
    )
    angles = positions.astype(jnp.float32)[:, :, None] * inv_freq
    cosine = jnp.cos(angles)[:, :, None, :]
    sine_part = signed * jnp.sin(angles)[:, :, None, :]
    front_half = values[..., :half_dim]
    back_half = values[..., half_dim:]
    return jnp.concatenate(
        [front_half * cosine - back_half * sine_part, back_half * cosine + front_half * sine_part],
        axis=-1,
    )


def norm_forward(values, gain_vec):
    scaled = lax.rsqrt(jnp.mean(values * values, axis=-1, keepdims=True) + EPSILON)
    normed = values * scaled
    return (normed, scaled, normed * gain_vec)


def norm_backward(upstream, normed, scaled, gain_vec):
    inner_grad = upstream * gain_vec
    back_grad = scaled * (
        inner_grad - normed * jnp.mean(inner_grad * normed, axis=-1, keepdims=True)
    )
    return (back_grad, jnp.sum(upstream * normed, axis=(0, 1)))


def state_summary(doc_ids, positions, inner_act, b_vec, step_size, log_keep):
    piece_len = inner_act.shape[1]
    cum_keep = running_sum(log_keep)
    drive_in = inner_act * step_size[..., None]
    tail_rate = jnp.where(
        (doc_ids == doc_ids[:, -1:])[:, :, None], jnp.exp(cum_keep[:, -1:, :] - cum_keep), 0.0
    )
    fresh_state = jnp.einsum("rsh,rshp,rsn->rhpn", tail_rate, drive_in, b_vec, precision=PRECISE)
    keep_rate = jnp.where(positions[:, -1:] > piece_len - 1, jnp.exp(cum_keep[:, -1]), 0.0)
    return (fresh_state, keep_rate)


def state_output(doc_ids, positions, inner_act, b_vec, c_vec, step_size, log_keep, entering):
    piece_len = inner_act.shape[1]
    local_place = jnp.arange(piece_len, dtype=jnp.int32)
    cum_keep = running_sum(log_keep)
    causal_mask = (local_place[:, None] >= local_place[None, :])[None] & (
        doc_ids[:, :, None] == doc_ids[:, None, :]
    )
    gap_log = cum_keep[:, :, None, :] - cum_keep[:, None, :, :]
    decay_mat = jnp.where(
        causal_mask[..., None], jnp.exp(jnp.where(causal_mask[..., None], gap_log, 0.0)), 0.0
    )
    gram_mat = jnp.einsum("rtn,rsn->rts", c_vec, b_vec, precision=PRECISE)
    drive_in = inner_act * step_size[..., None]
    state_out = jnp.einsum(
        "rtsh,rshp->rthp", gram_mat[..., None] * decay_mat, drive_in, precision=PRECISE
    )
    lift_rate = jnp.where((positions > local_place)[:, :, None], jnp.exp(cum_keep), 0.0)
    return (
        state_out
        + jnp.einsum("rtn,rhpn->rthp", c_vec, entering, precision=PRECISE) * lift_rate[..., None]
    )


def inner_dot(left, right):
    return lax.dot_general(left, right, (((1,), (1,)), ((), ())), preferred_element_type=jnp.float32)


def attend_kernel(span, low_ref, high_ref, query_ref, place_ref, begin_ref, kv_ref, kvt_ref, out_ref, stat_ref):
    row = pl.program_id(0)
    dim = query_ref.shape[2]
    width = query_ref.shape[1]
    query = query_ref[0]
    place = place_ref[0]
    begin = begin_ref[0]

    def step(block, carry):
        top, total, acc = carry
        at = pl.multiple_of(block * span, span)
        key = kv_ref[0, pl.ds(at, span), :dim]
        value_t = kvt_ref[0, dim:, pl.ds(at, span)]
        scores = inner_dot(key, query)
        key_place = at + lax.broadcasted_iota(jnp.int32, scores.shape, 0)
        allowed = (key_place <= place) & (key_place >= begin)
        scores = jnp.where(allowed, scores, FLOOR_SCORE)
        new_top = jnp.maximum(top, jnp.max(scores, axis=0, keepdims=True))
        probs = jnp.exp(scores - new_top)
        scale = jnp.exp(top - new_top)
        total = total * scale + jnp.sum(probs, axis=0, keepdims=True)
        acc = acc * scale + jnp.dot(
            value_t, probs.astype(jnp.bfloat16), preferred_element_type=jnp.float32
        )
        return new_top, total, acc

    top, total, acc = lax.fori_loop(
        low_ref[row],
        high_ref[row],
        step,
        (
            jnp.full((1, width), FIRST_TOP, jnp.float32),
            jnp.zeros((1, width), jnp.float32),
            jnp.zeros((dim, width), jnp.float32),
        ),
    )
    out_ref[0] = acc / total
    stat_ref[0] = top + jnp.log(total)


def attend_back_kernel(
    span, low_ref, high_ref, query_ref, grad_ref, place_ref, begin_ref, stat_ref, dot_ref, kv_ref, kvt_ref,
    query_grad_ref, kv_grad_ref,
):
    row = pl.program_id(0)
    dim = query_ref.shape[2]
    width = query_ref.shape[1]
    query = query_ref[0]
    grad = grad_ref[0]
    place = place_ref[0]
    begin = begin_ref[0]
    stat = stat_ref[0]
    dots = dot_ref[0]
    kv_grad_ref[...] = jnp.zeros_like(kv_grad_ref)

    def step(block, query_grad):
        at = pl.multiple_of(block * span, span)
        key = kv_ref[0, pl.ds(at, span), :dim]
        value = kv_ref[0, pl.ds(at, span), dim:]
        key_t = kvt_ref[0, :dim, pl.ds(at, span)]
        scores = inner_dot(key, query)
        key_place = at + lax.broadcasted_iota(jnp.int32, scores.shape, 0)
        allowed = (key_place <= place) & (key_place >= begin)
        probs = jnp.exp(jnp.where(allowed, scores - stat, FLOOR_SCORE))
        prob_grad = inner_dot(value, grad)
        score_grad = (probs * (prob_grad - dots)).astype(jnp.bfloat16)
        value_grad = jnp.dot(probs.astype(jnp.bfloat16), grad, preferred_element_type=jnp.float32)
        key_grad = jnp.dot(score_grad, query, preferred_element_type=jnp.float32)
        kv_grad_ref[0, pl.ds(at, span), :] = jnp.concatenate(
            [key_grad, value_grad], axis=1
        ).astype(jnp.bfloat16)
        return query_grad + jnp.dot(key_t, score_grad, preferred_element_type=jnp.float32)

    query_grad_ref[0] = lax.fori_loop(
        low_ref[row], high_ref[row], step, jnp.zeros((dim, width), jnp.float32)
    )


def row_spec(*shape):
    return pl.BlockSpec((1,) + shape, lambda r, *_: (r,) + (0,) * len(shape))


def attend_forward(span, low, high, query, place, begin, keyval, keyval_t):
    rows, width, dim = query.shape
    full = keyval.shape[1]
    return pl.pallas_call(
        partial(attend_kernel, span),
        grid_spec=pltpu.PrefetchScalarGridSpec(
            num_scalar_prefetch=2,
            grid=(rows,),
            in_specs=[
                row_spec(width, dim), row_spec(1, width), row_spec(1, width),
                row_spec(full, 2 * dim), row_spec(2 * dim, full),
            ],
            out_specs=[row_spec(dim, width), row_spec(1, width)],
        ),
        out_shape=[
            jax.ShapeDtypeStruct((rows, dim, width), jnp.float32),
            jax.ShapeDtypeStruct((rows, 1, width), jnp.float32),
        ],
        compiler_params=pltpu.CompilerParams(vmem_limit_bytes=48 * 1024 * 1024),
    )(low, high, query, place, begin, keyval, keyval_t)


def attend_backward(span, low, high, query, grad, place, begin, stat, dots, keyval, keyval_t):
    rows, width, dim = query.shape
    full = keyval.shape[1]
    return pl.pallas_call(
        partial(attend_back_kernel, span),
        grid_spec=pltpu.PrefetchScalarGridSpec(
            num_scalar_prefetch=2,
            grid=(rows,),
            in_specs=[
                row_spec(width, dim), row_spec(width, dim), row_spec(1, width), row_spec(1, width),
                row_spec(1, width), row_spec(1, width),
                row_spec(full, 2 * dim), row_spec(2 * dim, full),
            ],
            out_specs=[row_spec(dim, width), row_spec(full, 2 * dim)],
        ),
        out_shape=[
            jax.ShapeDtypeStruct((rows, dim, width), jnp.float32),
            jax.ShapeDtypeStruct((rows, full, 2 * dim), jnp.bfloat16),
        ],
        compiler_params=pltpu.CompilerParams(vmem_limit_bytes=48 * 1024 * 1024),
    )(low, high, query, grad, place, begin, stat, dots, keyval, keyval_t)


def head_kernel(ways, scatter, gather, part_ref, out_ref, landed, sends, arrivals):
    me = lax.axis_index("head")
    rows = part_ref.shape[0]
    share = part_ref.shape[1] // ways if scatter else part_ref.shape[1]
    barrier = pltpu.get_barrier_semaphore()
    for hop in range(1, ways):
        pl.semaphore_signal(
            barrier,
            inc=1,
            device_id={"head": lax.rem(me + hop, ways)},
            device_id_type=pl.DeviceIdType.MESH,
        )
    pl.semaphore_wait(barrier, ways - 1)
    mine = pl.ds(pl.multiple_of(me * share, 16), share)
    order = (2, 1, 3) if ways == 4 else tuple(range(1, ways))
    if scatter:
        copies = []
        for hop in order:
            peer = lax.rem(me + hop, ways)
            copy = pltpu.make_async_remote_copy(
                src_ref=part_ref.at[:, pl.ds(pl.multiple_of(peer * share, 16), share), :],
                dst_ref=landed.at[hop - 1],
                send_sem=sends.at[hop - 1],
                recv_sem=arrivals.at[hop - 1],
                device_id={"head": peer},
                device_id_type=pl.DeviceIdType.MESH,
            )
            copy.start()
            copies.append(copy)
        for copy in copies:
            copy.wait()
        place = mine if gather else pl.ds(0, share)
        for row in range(rows):
            total = part_ref[row, mine, :].astype(jnp.float32)
            for hop in range(1, ways):
                total = total + landed[hop - 1, row].astype(jnp.float32)
            out_ref[row, place, :] = total.astype(out_ref.dtype)
    else:
        for row in range(rows):
            out_ref[row, mine, :] = part_ref[row]
    if gather:
        copies = []
        for hop in order:
            copy = pltpu.make_async_remote_copy(
                src_ref=out_ref.at[:, mine, :],
                dst_ref=out_ref.at[:, mine, :],
                send_sem=sends.at[ways + hop - 1],
                recv_sem=arrivals.at[ways + hop - 1],
                device_id={"head": lax.rem(me + hop, ways)},
                device_id_type=pl.DeviceIdType.MESH,
            )
            copy.start()
            copies.append(copy)
        for copy in copies:
            copy.wait()


def head_exchange(part, number, scatter, gather):
    ways = lax.axis_size("head")
    rows, length, width = part.shape
    share = length // ways if scatter else length
    landed = (ways - 1, rows, share, width) if scatter else (1, 1, 16, 128)
    return pl.pallas_call(
        partial(head_kernel, ways, scatter, gather),
        out_shape=jax.ShapeDtypeStruct((rows, share * ways if gather else share, width), part.dtype),
        in_specs=[pl.BlockSpec(memory_space=pltpu.VMEM)],
        out_specs=pl.BlockSpec(memory_space=pltpu.VMEM),
        scratch_shapes=[
            pltpu.VMEM(landed, part.dtype),
            pltpu.SemaphoreType.DMA((2 * ways,)),
            pltpu.SemaphoreType.DMA((2 * ways,)),
        ],
        compiler_params=pltpu.CompilerParams(
            collective_id=number, has_side_effects=True, vmem_limit_bytes=32 * 1024 * 1024
        ),
    )(part)


def grads_kernel(ways, part_ref, out_ref, paired, landed, spread, sends, arrivals):
    me = lax.axis_index("seq")
    core = lax.rem(me, 2)
    chips = ways // 2
    chip = me // 2
    sibling = me + 1 - 2 * core
    half = part_ref.shape[0] // 2
    share = half // chips
    barrier = pltpu.get_barrier_semaphore()
    peers = [lax.rem(chip + hop, chips) * 2 + core for hop in range(1, chips)]
    for peer in peers + [sibling]:
        pl.semaphore_signal(
            barrier, inc=1, device_id={"seq": peer}, device_id_type=pl.DeviceIdType.MESH
        )
    pl.semaphore_wait(barrier, chips)

    def send(source, target, number, peer):
        copy = pltpu.make_async_remote_copy(
            src_ref=source,
            dst_ref=target,
            send_sem=sends.at[number],
            recv_sem=arrivals.at[number],
            device_id={"seq": peer},
            device_id_type=pl.DeviceIdType.MESH,
        )
        copy.start()
        return copy

    def span(start, size):
        return pl.ds(pl.multiple_of(start, 16), size)

    own = core * half
    send(part_ref.at[span((1 - core) * half, half), :], landed, 0, sibling).wait()

    @pl.loop(0, half // 16)
    def _(tile):
        here = span(tile * 16, 16)
        paired[here, :] = (
            part_ref[span(own + tile * 16, 16), :].astype(jnp.float32)
            + landed[here, :].astype(jnp.float32)
        ).astype(paired.dtype)

    copies = []
    for hop in range(1, chips):
        to = lax.rem(chip + hop, chips)
        copies.append(
            send(paired.at[span(to * share, share), :], spread.at[hop - 1], hop, peers[hop - 1])
        )
    for copy in copies:
        copy.wait()
    mine = own + chip * share

    @pl.loop(0, share // 16)
    def _(tile):
        here = span(tile * 16, 16)
        total = paired[span(chip * share + tile * 16, 16), :].astype(jnp.float32)
        for hop in range(1, chips):
            total = total + spread[hop - 1, here, :].astype(jnp.float32)
        out_ref[span(mine + tile * 16, 16), :] = total.astype(out_ref.dtype)

    place = out_ref.at[span(mine, share), :]
    copies = [
        send(place, place, chips + hop, peers[hop - 1]) for hop in range(1, chips)
    ]
    for copy in copies:
        copy.wait()
    place = out_ref.at[span(own, half), :]
    send(place, place, chips, sibling).wait()


def grads_sum(part, number):
    ways = lax.axis_size("seq")
    rows, width = part.shape
    chips = ways // 2
    return pl.pallas_call(
        partial(grads_kernel, ways),
        out_shape=jax.ShapeDtypeStruct(part.shape, part.dtype),
        in_specs=[pl.BlockSpec(memory_space=pltpu.VMEM)],
        out_specs=pl.BlockSpec(memory_space=pltpu.VMEM),
        scratch_shapes=[
            pltpu.VMEM((rows // 2, width), part.dtype),
            pltpu.VMEM((rows // 2, width), part.dtype),
            pltpu.VMEM((chips - 1, rows // ways, width), part.dtype),
            pltpu.SemaphoreType.DMA((2 * chips,)),
            pltpu.SemaphoreType.DMA((2 * chips,)),
        ],
        compiler_params=pltpu.CompilerParams(
            collective_id=number, has_side_effects=True, vmem_limit_bytes=48 * 1024 * 1024
        ),
    )(part)


def local(
    tokens,
    cotangent,
    doc_starts,
    norm_gain,
    mixer_proj,
    state_proj,
    step_proj,
    step_bias,
    decay_log,
    skip_gain,
    conv_mixer,
    conv_state,
    mixer_down,
    query_proj,
    keyval_proj,
    attend_down,
    ffn_gain,
    ffn_in,
    ffn_down,
):
    row_count, length, model_width = tokens.shape
    offset = lax.axis_index("seq") * length
    head_ways = lax.axis_size("head")
    share_len = length // head_ways
    share_start = lax.axis_index("head") * share_len
    inner_width = mixer_proj.shape[2]
    head_count = step_bias.shape[0]
    head_dim = inner_width // head_count
    states = state_proj.shape[1] // 2
    tap_count = conv_mixer.shape[0]
    local_heads = query_proj.shape[1] // ATT_DIM
    kv_total = keyval_proj.shape[2] // ATT_DIM
    group_size = ATT_HEADS // KV_HEADS
    kv_index = lax.axis_index("head") * local_heads // group_size
    score_scale = ATT_DIM ** (-0.5)
    doc_ids, positions = doc_layout(doc_starts, offset, length)
    places = jnp.arange(length, dtype=jnp.int32)

    def share_of(values):
        return lax.dynamic_slice_in_dim(values, share_start, share_len, 1)

    inputs = tokens.astype(jnp.float32)
    normed_one, scaled_one, gained_one = norm_forward(inputs, norm_gain)
    normed_low = gained_one.astype(jnp.bfloat16)
    mixer_pre = jnp.einsum(
        "rtd,dkc->rtkc", normed_low, mixer_proj, preferred_element_type=jnp.float32
    )
    gate_view = mixer_pre[:, :, 0].reshape(row_count, length, head_count, head_dim)
    state_pre = jnp.einsum(
        "rtd,dc->rtc", normed_low, state_proj, preferred_element_type=jnp.float32
    )
    step_pre = jnp.einsum("rtd,dh->rth", normed_low, step_proj, preferred_element_type=jnp.float32)
    query_pre = jnp.einsum(
        "rtd,dc->rtc", normed_low, query_proj, preferred_element_type=jnp.float32
    )
    keyval_mine = lax.dynamic_slice_in_dim(keyval_proj, kv_index * ATT_DIM, ATT_DIM, 2)
    keyval_pre = jnp.einsum(
        "rtd,dkc->rtkc", normed_low, keyval_mine, preferred_element_type=jnp.float32
    )
    conv_input = jnp.concatenate([mixer_pre[:, :, 1], state_pre], axis=2).astype(jnp.bfloat16)
    conv_weight = jnp.concatenate([conv_mixer, conv_state], axis=1)
    before = shifted(conv_input[:, length - (tap_count - 1) :], "seq", 1)
    padded = jnp.concatenate([before, conv_input], axis=1)
    conv_pre = jnp.zeros(conv_input.shape, jnp.float32)
    for tap_index in range(tap_count):
        lag_steps = tap_count - 1 - tap_index
        conv_pre = conv_pre + jnp.where(
            (positions >= lag_steps)[:, :, None],
            padded[:, tap_index : tap_index + length] * conv_weight[tap_index],
            0.0,
        )
    activated = silu_value(conv_pre).astype(jnp.bfloat16)
    mixer_act = (
        activated[:, :, :inner_width]
        .reshape(row_count, length, head_count, head_dim)
        .astype(jnp.float32)
    )
    state_b = activated[:, :, inner_width : inner_width + states].astype(jnp.float32)
    state_c = activated[:, :, inner_width + states :].astype(jnp.float32)
    step_size = jax.nn.softplus(step_pre + step_bias)
    decay_rates = jnp.exp(decay_log)
    log_keep = -step_size * decay_rates
    (fresh_state, keep_rate), summary_back = jax.vjp(
        partial(state_summary, doc_ids, positions), mixer_act, state_b, step_size, log_keep
    )
    seq_index = lax.axis_index("seq")
    all_keep = lax.all_gather(keep_rate.astype(jnp.bfloat16), "seq")
    entering = carried_in(
        all_keep, lax.all_gather(fresh_state.astype(jnp.bfloat16), "seq"), seq_index, False
    )
    mixed_state, output_back = jax.vjp(
        partial(state_output, doc_ids, positions),
        mixer_act,
        state_b,
        state_c,
        step_size,
        log_keep,
        entering,
    )
    full_state = mixed_state + skip_gain[:, None] * mixer_act
    gated_low = (
        (full_state * silu_value(gate_view))
        .reshape(row_count, length, inner_width)
        .astype(jnp.bfloat16)
    )
    mixer_part = jnp.einsum(
        "rtc,cd->rtd", gated_low, mixer_down, preferred_element_type=jnp.float32
    )
    query_rot = rotate(
        query_pre.reshape(row_count, length, local_heads, ATT_DIM), positions, 1.0
    ).astype(jnp.bfloat16)
    key_rot = rotate(keyval_pre[:, :, 0][:, :, None], positions, 1.0)[:, :, 0].astype(jnp.bfloat16)
    value_low = keyval_pre[:, :, 1].astype(jnp.bfloat16)
    keyval_all = lax.all_gather(
        jnp.concatenate([key_rot, value_low], axis=2), "seq", axis=1, tiled=True
    )
    keyval_t = jnp.swapaxes(keyval_all, 1, 2)
    query_scaled = (
        jnp.swapaxes(query_rot, 1, 2).reshape(row_count, local_heads * length, ATT_DIM)
        * jnp.bfloat16(score_scale)
    )
    begins = offset + places[None, :] - positions
    place_row = jnp.tile(offset + places, local_heads)[None, None, :]
    place_row = jnp.broadcast_to(place_row, (row_count, 1, local_heads * length))
    begin_row = jnp.tile(begins, (1, local_heads))[:, None, :]
    low_block = begins[:, 0] // length
    high_block = jnp.broadcast_to(lax.axis_index("seq") + 1, (row_count,)).astype(jnp.int32)
    attended_t, stat_row = attend_forward(
        length, low_block, high_block, query_scaled, place_row, begin_row, keyval_all, keyval_t
    )
    attended = attended_t.reshape(row_count, ATT_DIM, local_heads, length).transpose(0, 3, 2, 1)
    attended_low = attended.astype(jnp.bfloat16).reshape(row_count, length, local_heads * ATT_DIM)
    attend_part = jnp.einsum(
        "rtc,cd->rtd", attended_low, attend_down, preferred_element_type=jnp.float32
    )
    mixed_sum = head_exchange(
        (mixer_part + attend_part).astype(jnp.bfloat16), 1, True, True
    ).astype(jnp.float32)
    middle = inputs + mixed_sum
    normed_two, scaled_two, gained_two = norm_forward(middle, ffn_gain)
    middle_low = gained_two.astype(jnp.bfloat16)
    ffn_pre = jnp.einsum("rtd,dkf->rtkf", middle_low, ffn_in, preferred_element_type=jnp.float32)
    hidden = (silu_value(ffn_pre[:, :, 0]) * ffn_pre[:, :, 1]).astype(jnp.bfloat16)
    ffn_part = jnp.einsum("rtf,fd->rtd", hidden, ffn_down, preferred_element_type=jnp.float32)
    ffn_share_sum = lax.psum_scatter(
        ffn_part.astype(jnp.bfloat16), "head", scatter_dimension=1, tiled=True
    ).astype(jnp.float32)
    output_share = (share_of(middle) + ffn_share_sum).astype(jnp.bfloat16)
    hidden_grad = jnp.einsum("rtd,fd->rtf", cotangent, ffn_down, preferred_element_type=jnp.float32)
    ffn_down_grad = jnp.einsum("rtf,rtd->fd", hidden, cotangent, preferred_element_type=jnp.float32)
    gate_value = ffn_pre[:, :, 0]
    ffn_pre_grad = jnp.stack(
        [
            hidden_grad * ffn_pre[:, :, 1] * silu_slope(gate_value),
            hidden_grad * silu_value(gate_value),
        ],
        axis=2,
    ).astype(jnp.bfloat16)
    ffn_in_grad = jnp.einsum(
        "rtd,rtkf->dkf", middle_low, ffn_pre_grad, preferred_element_type=jnp.float32
    )
    middle_low_part = jnp.einsum(
        "rtkf,dkf->rtd", ffn_pre_grad, ffn_in, preferred_element_type=jnp.float32
    )
    low_grad_share = head_exchange(
        middle_low_part.astype(jnp.bfloat16), 2, True, False
    ).astype(jnp.float32)
    norm_back_share, ffn_gain_part = norm_backward(
        low_grad_share, share_of(normed_two), share_of(scaled_two), ffn_gain
    )
    middle_grad_share = share_of(cotangent).astype(jnp.float32) + norm_back_share
    mixed_low = head_exchange(middle_grad_share.astype(jnp.bfloat16), 3, False, True)
    gated_grad = jnp.einsum(
        "rtd,cd->rtc", mixed_low, mixer_down, preferred_element_type=jnp.float32
    ).reshape(row_count, length, head_count, head_dim)
    mixer_down_grad = jnp.einsum(
        "rtc,rtd->cd", gated_low, mixed_low, preferred_element_type=jnp.float32
    )
    attended_grad = jnp.einsum(
        "rtd,cd->rtc", mixed_low, attend_down, preferred_element_type=jnp.float32
    ).astype(jnp.bfloat16)
    attend_down_grad = jnp.einsum(
        "rtc,rtd->cd", attended_low, mixed_low, preferred_element_type=jnp.float32
    )
    attended_grad = attended_grad.reshape(row_count, length, local_heads, ATT_DIM)
    grad_dot = jnp.swapaxes(jnp.sum(attended_grad.astype(jnp.float32) * attended, axis=-1), 1, 2)

    query_grad_t, keyval_grads = attend_backward(
        length,
        low_block,
        high_block,
        query_scaled,
        jnp.swapaxes(attended_grad, 1, 2).reshape(row_count, local_heads * length, ATT_DIM),
        place_row,
        begin_row,
        stat_row,
        grad_dot.reshape(row_count, 1, local_heads * length),
        keyval_all,
        keyval_t,
    )
    query_grad = (
        query_grad_t.reshape(row_count, ATT_DIM, local_heads, length).transpose(0, 3, 2, 1)
        * score_scale
    )
    keyval_grad = lax.psum_scatter(
        keyval_grads, "seq", scatter_dimension=1, tiled=True
    ).astype(jnp.float32)
    key_grad, value_grad = keyval_grad[..., :ATT_DIM], keyval_grad[..., ATT_DIM:]
    query_low = (
        rotate(query_grad, positions, -1.0)
        .reshape(row_count, length, local_heads * ATT_DIM)
        .astype(jnp.bfloat16)
    )
    keyval_own = jnp.stack(
        [rotate(key_grad[:, :, None], positions, -1.0)[:, :, 0], value_grad], axis=2
    )
    keyval_part = jnp.zeros((row_count, length, 2, kv_total, ATT_DIM), jnp.float32)
    keyval_part = lax.dynamic_update_slice_in_dim(
        keyval_part, keyval_own[:, :, :, None], kv_index, 3
    )
    state_grad = gated_grad * silu_value(gate_view)
    gate_grad = gated_grad * full_state * silu_slope(gate_view)
    skip_gain_grad = jnp.sum(state_grad * mixer_act, axis=(0, 1, 3))
    lift_rate = jnp.where(
        (positions > places)[:, :, None], jnp.exp(running_sum(log_keep)), 0.0
    )
    local_grad = jnp.einsum(
        "rthp,rtn->rhpn", state_grad * lift_rate[..., None], state_c, precision=PRECISE
    )
    after_grad = carried_in(
        all_keep, lax.all_gather(local_grad.astype(jnp.bfloat16), "seq"), seq_index, True
    )
    keep_grad = jnp.sum(after_grad * entering, axis=(2, 3))
    act_grad_one, b_grad_one, step_grad_one, log_grad_one = summary_back((after_grad, keep_grad))
    act_grad_two, b_grad_two, c_grad, step_grad_two, log_grad_two, entering_grad = output_back(
        state_grad
    )
    mixer_act_grad = act_grad_one + act_grad_two + state_grad * skip_gain[:, None]
    log_grad = log_grad_one + log_grad_two
    step_grad = step_grad_one + step_grad_two - log_grad * decay_rates
    decay_log_grad = jnp.sum(log_grad * log_keep, axis=(0, 1))
    step_pre_grad = step_grad * jax.nn.sigmoid(step_pre + step_bias)
    step_bias_grad = jnp.sum(step_pre_grad, axis=(0, 1))
    step_low = step_pre_grad.astype(jnp.bfloat16)
    act_grad = jnp.concatenate(
        [mixer_act_grad.reshape(row_count, length, inner_width), b_grad_one + b_grad_two, c_grad],
        axis=2,
    )
    pre_grad = act_grad * silu_slope(conv_pre)
    state_width = pre_grad.shape[2] - inner_width
    shared_total = head_exchange(
        jnp.concatenate(
            [
                pre_grad[:, :, inner_width:].astype(jnp.bfloat16),
                keyval_part.reshape(row_count, length, 2 * kv_total * ATT_DIM).astype(jnp.bfloat16),
            ],
            axis=2,
        ),
        4,
        True,
        True,
    ).astype(jnp.float32)
    state_total, keyval_total = shared_total[..., :state_width], shared_total[..., state_width:]
    pre_grad = jnp.concatenate([pre_grad[:, :, :inner_width], state_total], axis=2)
    padded_grad = jnp.zeros((row_count, length + tap_count - 1, pre_grad.shape[2]), jnp.float32)
    conv_grads = []
    for tap_index in range(tap_count):
        lag_steps = tap_count - 1 - tap_index
        masked = jnp.where((positions >= lag_steps)[:, :, None], pre_grad, 0.0)
        conv_grads.append(jnp.sum(masked * padded[:, tap_index : tap_index + length], axis=(0, 1)))
        padded_grad = padded_grad + jnp.pad(
            masked * conv_weight[tap_index], ((0, 0), (tap_index, lag_steps), (0, 0))
        )
    conv_weight_grad = jnp.stack(conv_grads, axis=0)
    rim_grad = shifted(padded_grad[:, : tap_count - 1], "seq", -1)
    conv_input_grad = padded_grad[:, tap_count - 1 :] + jnp.pad(
        rim_grad, ((0, 0), (length - (tap_count - 1), 0), (0, 0))
    )
    mixer_low = jnp.stack(
        [gate_grad.reshape(row_count, length, inner_width), conv_input_grad[:, :, :inner_width]],
        axis=2,
    ).astype(jnp.bfloat16)
    state_low = conv_input_grad[:, :, inner_width:].astype(jnp.bfloat16)
    keyval_low = keyval_total.reshape(row_count, length, 2, kv_total * ATT_DIM).astype(jnp.bfloat16)
    mixer_proj_grad = jnp.einsum(
        "rtd,rtkc->dkc", normed_low, mixer_low, preferred_element_type=jnp.float32
    )
    state_proj_grad = jnp.einsum(
        "rtd,rtc->dc", normed_low, state_low, preferred_element_type=jnp.float32
    )
    step_proj_grad = jnp.einsum(
        "rtd,rth->dh", normed_low, step_low, preferred_element_type=jnp.float32
    )
    query_proj_grad = jnp.einsum(
        "rtd,rtc->dc", normed_low, query_low, preferred_element_type=jnp.float32
    )
    keyval_proj_grad = jnp.einsum(
        "rtd,rtkc->dkc", normed_low, keyval_low, preferred_element_type=jnp.float32
    )
    head_part = (
        jnp.einsum("rtkc,dkc->rtd", mixer_low, mixer_proj, preferred_element_type=jnp.float32)
        + jnp.einsum("rth,dh->rtd", step_low, step_proj, preferred_element_type=jnp.float32)
        + jnp.einsum("rtc,dc->rtd", query_low, query_proj, preferred_element_type=jnp.float32)
    )
    common_share = jnp.einsum(
        "rtc,dc->rtd", share_of(state_low), state_proj, preferred_element_type=jnp.float32
    ) + jnp.einsum(
        "rtkc,dkc->rtd", share_of(keyval_low), keyval_proj, preferred_element_type=jnp.float32
    )
    normed_share = share_of(normed_one)
    norm_rider = jnp.sum(head_part * normed_one, axis=(0, 1)) + jnp.sum(
        common_share * normed_share, axis=(0, 1)
    )
    head_share = head_exchange(head_part.astype(jnp.bfloat16), 5, True, False).astype(jnp.float32)
    gains = jnp.pad(
        jnp.stack([ffn_gain_part, norm_rider]).astype(jnp.bfloat16)[None], ((0, 0), (0, 14), (0, 0))
    )
    gains = jnp.sum(
        head_exchange(gains, 6, False, True)
        .astype(jnp.float32)
        .reshape(head_ways, 16, model_width)[:, :2],
        axis=0,
    )
    norm_back_share_one, unused_gain = norm_backward(
        head_share + common_share, normed_share, share_of(scaled_one), norm_gain
    )
    token_share = (middle_grad_share + norm_back_share_one).astype(jnp.bfloat16)
    output, token_grad = (
        lax.all_gather(output_share, "head", axis=1, tiled=True),
        head_exchange(token_share, 7, False, True),
    )
    def tall(values):
        return jnp.pad(values, ((0, model_width - values.shape[0]), (0, 0)))

    small = [
        step_proj_grad,
        gains.T,
        tall(conv_weight_grad[:, :inner_width].T),
        tall(conv_weight_grad[:, inner_width:].T),
        tall(jnp.stack([step_bias_grad, decay_log_grad, skip_gain_grad], axis=1)),
    ]
    small = jnp.concatenate(small, axis=1)
    small = jnp.pad(small, ((0, 0), (0, 128 - small.shape[1])))
    down_grads = [ffn_down_grad, mixer_down_grad, attend_down_grad]
    pieces = [
        mixer_proj_grad.reshape(model_width, -1),
        ffn_in_grad.reshape(model_width, -1),
        query_proj_grad,
        state_proj_grad,
        keyval_proj_grad.reshape(model_width, -1),
        tall(jnp.concatenate([grad.astype(jnp.bfloat16) for grad in down_grads], axis=0)),
        small,
    ]
    summed = grads_sum(jnp.concatenate([piece.astype(jnp.bfloat16) for piece in pieces], axis=1), 8)
    parts = []
    begin = 0
    for piece in pieces:
        parts.append(summed[:, begin : begin + piece.shape[1]].astype(jnp.float32))
        begin += piece.shape[1]
    mixer_proj_sum = parts[0].reshape(mixer_proj_grad.shape)
    ffn_in_sum = parts[1].reshape(ffn_in_grad.shape)
    query_proj_sum, state_proj_sum = parts[2], parts[3]
    keyval_proj_sum = parts[4].reshape(keyval_proj_grad.shape)
    down_at = (ffn_down_grad.shape[0], ffn_down_grad.shape[0] + mixer_down_grad.shape[0])
    ffn_down_sum, mixer_down_sum, attend_down_sum = jnp.split(
        parts[5][: down_at[1] + attend_down_grad.shape[0]], down_at, axis=0
    )
    small_sum = parts[6]
    at = head_count
    step_proj_sum = small_sum[:, :at]
    ffn_gain_sum, norm_gain_sum = small_sum[:, at], small_sum[:, at + 1]
    at += 2
    conv_mixer_sum = small_sum[:inner_width, at : at + tap_count].T
    at += tap_count
    conv_state_sum = small_sum[: 2 * states, at : at + tap_count].T
    at += tap_count
    step_bias_sum, decay_log_sum, skip_gain_sum = (small_sum[:head_count, at + i] for i in range(3))
    return (
        output,
        token_grad,
        norm_gain_sum,
        mixer_proj_sum,
        state_proj_sum,
        step_proj_sum,
        step_bias_sum,
        decay_log_sum,
        skip_gain_sum,
        conv_mixer_sum,
        conv_state_sum,
        mixer_down_sum,
        query_proj_sum,
        keyval_proj_sum,
        attend_down_sum,
        ffn_gain_sum,
        ffn_in_sum,
        ffn_down_sum,
    )


def solution(mesh):
    placed = (
        P(None, "seq", None),
        P(None, "seq", None),
        P(),
        P(),
        P(None, None, "head"),
        P(),
        P(None, "head"),
        P("head"),
        P("head"),
        P("head"),
        P(None, "head"),
        P(),
        P("head", None),
        P(None, "head"),
        P(),
        P("head", None),
        P(),
        P(None, None, "head"),
        P("head", None),
    )
    return jax.shard_map(
        local,
        mesh=mesh,
        in_specs=placed,
        out_specs=(
            P(None, "seq", None),
            P(None, "seq", None),
            P(),
            P(None, None, "head"),
            P(),
            P(None, "head"),
            P("head"),
            P("head"),
            P("head"),
            P(None, "head"),
            P(),
            P("head", None),
            P(None, "head"),
            P(),
            P("head", None),
            P(),
            P(None, None, "head"),
            P("head", None),
        ),
        check_vma=False,
    )
```

```python
from functools import partial
import math

import jax
import jax.numpy as jnp
from jax import lax
from jax.experimental import pallas as pl
from jax.experimental.pallas import tpu as pltpu
from jax.sharding import PartitionSpec as P

ATT_HEADS = 8
KV_HEADS = 2
ATT_DIM = 64


EPSILON = 1e-05
PRECISE = lax.Precision.DEFAULT
ROPE_BASE = 10000.0
FLOOR_SCORE = -1e30
FIRST_TOP = -1e29


def shifted(block, axis, distance):
    devices = range(lax.axis_size(axis))
    route = [(i - distance, i) for i in devices if i - distance in devices]
    return lax.ppermute(block, axis, route)


def carried_in(keeps, states, index, reverse):
    size = keeps.shape[0]
    order = jnp.arange(size)
    source, between = order[:, None], order[None, :]
    if reverse:
        inside = (between < source) & (between > index)
        reached = order > index
    else:
        inside = (between > source) & (between < index)
        reached = order < index
    weight = jnp.prod(
        jnp.where(inside[:, :, None, None], keeps.astype(jnp.float32)[None], 1.0), axis=1
    )
    weight = jnp.where(reached[:, None, None], weight, 0.0)
    return jnp.sum(weight[..., None, None] * states.astype(jnp.float32), axis=0)


def running_sum(values):
    length = values.shape[1]
    steps = jnp.arange(length)
    lower = (steps[:, None] >= steps[None, :]).astype(jnp.float32)
    return jnp.einsum("ts,rsh->rth", lower, values, precision=lax.Precision.HIGHEST)


def silu_value(values):
    return values * jax.nn.sigmoid(values)


def silu_slope(values):
    logistic = jax.nn.sigmoid(values)
    return logistic * (1.0 + values * (1.0 - logistic))


def doc_layout(starts, offset, length):
    places = offset + jnp.arange(length, dtype=jnp.int32)
    passed = starts[:, None, :] <= places[None, :, None]
    doc_ids = jnp.sum(passed.astype(jnp.int32), axis=2)
    begins = jnp.max(jnp.where(passed, starts[:, None, :], 0), axis=2)
    return (doc_ids, places[None, :] - begins)


def rotate(values, positions, signed):
    half_dim = values.shape[-1] // 2
    inv_freq = jnp.exp(
        jnp.arange(half_dim).astype(jnp.float32) * (-2.0 * math.log(ROPE_BASE) / values.shape[-1])
    )
    angles = positions.astype(jnp.float32)[:, :, None] * inv_freq
    cosine = jnp.cos(angles)[:, :, None, :]
    sine_part = signed * jnp.sin(angles)[:, :, None, :]
    front_half = values[..., :half_dim]
    back_half = values[..., half_dim:]
    return jnp.concatenate(
        [front_half * cosine - back_half * sine_part, back_half * cosine + front_half * sine_part],
        axis=-1,
    )


def norm_forward(values, gain_vec):
    scaled = lax.rsqrt(jnp.mean(values * values, axis=-1, keepdims=True) + EPSILON)
    normed = values * scaled
    return (normed, scaled, normed * gain_vec)


def norm_backward(upstream, normed, scaled, gain_vec):
    inner_grad = upstream * gain_vec
    back_grad = scaled * (
        inner_grad - normed * jnp.mean(inner_grad * normed, axis=-1, keepdims=True)
    )
    return (back_grad, jnp.sum(upstream * normed, axis=(0, 1)))


def state_summary(doc_ids, positions, inner_act, b_vec, step_size, log_keep):
    piece_len = inner_act.shape[1]
    cum_keep = running_sum(log_keep)
    drive_in = inner_act * step_size[..., None]
    tail_rate = jnp.where(
        (doc_ids == doc_ids[:, -1:])[:, :, None], jnp.exp(cum_keep[:, -1:, :] - cum_keep), 0.0
    )
    fresh_state = jnp.einsum("rsh,rshp,rsn->rhpn", tail_rate, drive_in, b_vec, precision=PRECISE)
    keep_rate = jnp.where(positions[:, -1:] > piece_len - 1, jnp.exp(cum_keep[:, -1]), 0.0)
    return (fresh_state, keep_rate)


def state_output(doc_ids, positions, inner_act, b_vec, c_vec, step_size, log_keep, entering):
    piece_len = inner_act.shape[1]
    local_place = jnp.arange(piece_len, dtype=jnp.int32)
    cum_keep = running_sum(log_keep)
    causal_mask = (local_place[:, None] >= local_place[None, :])[None] & (
        doc_ids[:, :, None] == doc_ids[:, None, :]
    )
    gap_log = cum_keep[:, :, None, :] - cum_keep[:, None, :, :]
    decay_mat = jnp.where(
        causal_mask[..., None], jnp.exp(jnp.where(causal_mask[..., None], gap_log, 0.0)), 0.0
    )
    gram_mat = jnp.einsum("rtn,rsn->rts", c_vec, b_vec, precision=PRECISE)
    drive_in = inner_act * step_size[..., None]
    state_out = jnp.einsum(
        "rtsh,rshp->rthp", gram_mat[..., None] * decay_mat, drive_in, precision=PRECISE
    )
    lift_rate = jnp.where((positions > local_place)[:, :, None], jnp.exp(cum_keep), 0.0)
    return (
        state_out
        + jnp.einsum("rtn,rhpn->rthp", c_vec, entering, precision=PRECISE) * lift_rate[..., None]
    )


def inner_dot(left, right):
    return lax.dot_general(left, right, (((1,), (1,)), ((), ())), preferred_element_type=jnp.float32)


def attend_kernel(span, low_ref, high_ref, query_ref, place_ref, begin_ref, kv_ref, kvt_ref, out_ref, stat_ref):
    row = pl.program_id(0)
    dim = query_ref.shape[2]
    width = query_ref.shape[1]
    query = query_ref[0]
    place = place_ref[0]
    begin = begin_ref[0]

    def step(block, carry):
        top, total, acc = carry
        at = pl.multiple_of(block * span, span)
        key = kv_ref[0, pl.ds(at, span), :dim]
        value_t = kvt_ref[0, dim:, pl.ds(at, span)]
        scores = inner_dot(key, query)
        key_place = at + lax.broadcasted_iota(jnp.int32, scores.shape, 0)
        allowed = (key_place <= place) & (key_place >= begin)
        scores = jnp.where(allowed, scores, FLOOR_SCORE)
        new_top = jnp.maximum(top, jnp.max(scores, axis=0, keepdims=True))
        probs = jnp.exp(scores - new_top)
        scale = jnp.exp(top - new_top)
        total = total * scale + jnp.sum(probs, axis=0, keepdims=True)
        acc = acc * scale + jnp.dot(
            value_t, probs.astype(jnp.bfloat16), preferred_element_type=jnp.float32
        )
        return new_top, total, acc

    top, total, acc = lax.fori_loop(
        low_ref[row],
        high_ref[row],
        step,
        (
            jnp.full((1, width), FIRST_TOP, jnp.float32),
            jnp.zeros((1, width), jnp.float32),
            jnp.zeros((dim, width), jnp.float32),
        ),
    )
    out_ref[0] = acc / total
    stat_ref[0] = top + jnp.log(total)


def attend_back_kernel(
    span, low_ref, high_ref, query_ref, grad_ref, place_ref, begin_ref, stat_ref, dot_ref, kv_ref, kvt_ref,
    query_grad_ref, kv_grad_ref,
):
    row = pl.program_id(0)
    dim = query_ref.shape[2]
    width = query_ref.shape[1]
    query = query_ref[0]
    grad = grad_ref[0]
    place = place_ref[0]
    begin = begin_ref[0]
    stat = stat_ref[0]
    dots = dot_ref[0]
    kv_grad_ref[...] = jnp.zeros_like(kv_grad_ref)

    def step(block, query_grad):
        at = pl.multiple_of(block * span, span)
        key = kv_ref[0, pl.ds(at, span), :dim]
        value = kv_ref[0, pl.ds(at, span), dim:]
        key_t = kvt_ref[0, :dim, pl.ds(at, span)]
        scores = inner_dot(key, query)
        key_place = at + lax.broadcasted_iota(jnp.int32, scores.shape, 0)
        allowed = (key_place <= place) & (key_place >= begin)
        probs = jnp.exp(jnp.where(allowed, scores - stat, FLOOR_SCORE))
        prob_grad = inner_dot(value, grad)
        score_grad = (probs * (prob_grad - dots)).astype(jnp.bfloat16)
        value_grad = jnp.dot(probs.astype(jnp.bfloat16), grad, preferred_element_type=jnp.float32)
        key_grad = jnp.dot(score_grad, query, preferred_element_type=jnp.float32)
        kv_grad_ref[0, pl.ds(at, span), :] = jnp.concatenate(
            [key_grad, value_grad], axis=1
        ).astype(jnp.bfloat16)
        return query_grad + jnp.dot(key_t, score_grad, preferred_element_type=jnp.float32)

    query_grad_ref[0] = lax.fori_loop(
        low_ref[row], high_ref[row], step, jnp.zeros((dim, width), jnp.float32)
    )


def row_spec(*shape):
    return pl.BlockSpec((1,) + shape, lambda r, *_: (r,) + (0,) * len(shape))


def attend_forward(span, low, high, query, place, begin, keyval, keyval_t):
    rows, width, dim = query.shape
    full = keyval.shape[1]
    return pl.pallas_call(
        partial(attend_kernel, span),
        grid_spec=pltpu.PrefetchScalarGridSpec(
            num_scalar_prefetch=2,
            grid=(rows,),
            in_specs=[
                row_spec(width, dim), row_spec(1, width), row_spec(1, width),
                row_spec(full, 2 * dim), row_spec(2 * dim, full),
            ],
            out_specs=[row_spec(dim, width), row_spec(1, width)],
        ),
        out_shape=[
            jax.ShapeDtypeStruct((rows, dim, width), jnp.float32),
            jax.ShapeDtypeStruct((rows, 1, width), jnp.float32),
        ],
        compiler_params=pltpu.CompilerParams(vmem_limit_bytes=48 * 1024 * 1024),
    )(low, high, query, place, begin, keyval, keyval_t)


def attend_backward(span, low, high, query, grad, place, begin, stat, dots, keyval, keyval_t):
    rows, width, dim = query.shape
    full = keyval.shape[1]
    return pl.pallas_call(
        partial(attend_back_kernel, span),
        grid_spec=pltpu.PrefetchScalarGridSpec(
            num_scalar_prefetch=2,
            grid=(rows,),
            in_specs=[
                row_spec(width, dim), row_spec(width, dim), row_spec(1, width), row_spec(1, width),
                row_spec(1, width), row_spec(1, width),
                row_spec(full, 2 * dim), row_spec(2 * dim, full),
            ],
            out_specs=[row_spec(dim, width), row_spec(full, 2 * dim)],
        ),
        out_shape=[
            jax.ShapeDtypeStruct((rows, dim, width), jnp.float32),
            jax.ShapeDtypeStruct((rows, full, 2 * dim), jnp.bfloat16),
        ],
        compiler_params=pltpu.CompilerParams(vmem_limit_bytes=48 * 1024 * 1024),
    )(low, high, query, grad, place, begin, stat, dots, keyval, keyval_t)


def grads_kernel(ways, part_ref, out_ref, paired, landed, spread, sends, arrivals):
    me = lax.axis_index("seq")
    core = lax.rem(me, 2)
    chips = ways // 2
    chip = me // 2
    sibling = me + 1 - 2 * core
    half = part_ref.shape[0] // 2
    share = half // chips
    barrier = pltpu.get_barrier_semaphore()
    peers = [lax.rem(chip + hop, chips) * 2 + core for hop in range(1, chips)]
    for peer in peers + [sibling]:
        pl.semaphore_signal(
            barrier, inc=1, device_id={"seq": peer}, device_id_type=pl.DeviceIdType.MESH
        )
    pl.semaphore_wait(barrier, chips)

    def send(source, target, number, peer):
        copy = pltpu.make_async_remote_copy(
            src_ref=source,
            dst_ref=target,
            send_sem=sends.at[number],
            recv_sem=arrivals.at[number],
            device_id={"seq": peer},
            device_id_type=pl.DeviceIdType.MESH,
        )
        copy.start()
        return copy

    def span(start, size):
        return pl.ds(pl.multiple_of(start, 16), size)

    own = core * half
    send(part_ref.at[span((1 - core) * half, half), :], landed, 0, sibling).wait()

    @pl.loop(0, half // 16)
    def _(tile):
        here = span(tile * 16, 16)
        paired[here, :] = (
            part_ref[span(own + tile * 16, 16), :].astype(jnp.float32)
            + landed[here, :].astype(jnp.float32)
        ).astype(paired.dtype)

    copies = []
    for hop in range(1, chips):
        to = lax.rem(chip + hop, chips)
        copies.append(
            send(paired.at[span(to * share, share), :], spread.at[hop - 1], hop, peers[hop - 1])
        )
    for copy in copies:
        copy.wait()
    mine = own + chip * share

    @pl.loop(0, share // 16)
    def _(tile):
        here = span(tile * 16, 16)
        total = paired[span(chip * share + tile * 16, 16), :].astype(jnp.float32)
        for hop in range(1, chips):
            total = total + spread[hop - 1, here, :].astype(jnp.float32)
        out_ref[span(mine + tile * 16, 16), :] = total.astype(out_ref.dtype)

    place = out_ref.at[span(mine, share), :]
    copies = [
        send(place, place, chips + hop, peers[hop - 1]) for hop in range(1, chips)
    ]
    for copy in copies:
        copy.wait()
    place = out_ref.at[span(own, half), :]
    send(place, place, chips, sibling).wait()


def grads_sum(part, number):
    ways = lax.axis_size("seq")
    rows, width = part.shape
    chips = ways // 2
    return pl.pallas_call(
        partial(grads_kernel, ways),
        out_shape=jax.ShapeDtypeStruct(part.shape, part.dtype),
        in_specs=[pl.BlockSpec(memory_space=pltpu.VMEM)],
        out_specs=pl.BlockSpec(memory_space=pltpu.VMEM),
        scratch_shapes=[
            pltpu.VMEM((rows // 2, width), part.dtype),
            pltpu.VMEM((rows // 2, width), part.dtype),
            pltpu.VMEM((chips - 1, rows // ways, width), part.dtype),
            pltpu.SemaphoreType.DMA((2 * chips,)),
            pltpu.SemaphoreType.DMA((2 * chips,)),
        ],
        cost_estimate=pl.CostEstimate(
            flops=2 * part.size, bytes_accessed=48 * part.size, transcendentals=0
        ),
        compiler_params=pltpu.CompilerParams(
            collective_id=number, has_side_effects=True, vmem_limit_bytes=32 * 1024 * 1024
        ),
    )(part)


def local(
    tokens,
    cotangent,
    doc_starts,
    norm_gain,
    mixer_proj,
    state_proj,
    step_proj,
    step_bias,
    decay_log,
    skip_gain,
    conv_mixer,
    conv_state,
    mixer_down,
    query_proj,
    keyval_proj,
    attend_down,
    ffn_gain,
    ffn_in,
    ffn_down,
):
    row_count, length, model_width = tokens.shape
    offset = lax.axis_index("seq") * length
    head_ways = lax.axis_size("head")
    share_len = length // head_ways
    share_start = lax.axis_index("head") * share_len
    inner_width = mixer_proj.shape[2]
    head_count = step_bias.shape[0]
    head_dim = inner_width // head_count
    states = state_proj.shape[1] // 2
    tap_count = conv_mixer.shape[0]
    local_heads = query_proj.shape[1] // ATT_DIM
    kv_total = keyval_proj.shape[2] // ATT_DIM
    group_size = ATT_HEADS // KV_HEADS
    kv_index = lax.axis_index("head") * local_heads // group_size
    score_scale = ATT_DIM ** (-0.5)
    doc_ids, positions = doc_layout(doc_starts, offset, length)
    places = jnp.arange(length, dtype=jnp.int32)

    def share_of(values):
        return lax.dynamic_slice_in_dim(values, share_start, share_len, 1)

    inputs = tokens.astype(jnp.float32)
    normed_one, scaled_one, gained_one = norm_forward(inputs, norm_gain)
    normed_low = gained_one.astype(jnp.bfloat16)
    mixer_pre = jnp.einsum(
        "rtd,dkc->rtkc", normed_low, mixer_proj, preferred_element_type=jnp.float32
    )
    gate_view = mixer_pre[:, :, 0].reshape(row_count, length, head_count, head_dim)
    state_pre = jnp.einsum(
        "rtd,dc->rtc", normed_low, state_proj, preferred_element_type=jnp.float32
    )
    step_pre = jnp.einsum("rtd,dh->rth", normed_low, step_proj, preferred_element_type=jnp.float32)
    query_pre = jnp.einsum(
        "rtd,dc->rtc", normed_low, query_proj, preferred_element_type=jnp.float32
    )
    keyval_mine = lax.dynamic_slice_in_dim(keyval_proj, kv_index * ATT_DIM, ATT_DIM, 2)
    keyval_pre = jnp.einsum(
        "rtd,dkc->rtkc", normed_low, keyval_mine, preferred_element_type=jnp.float32
    )
    conv_input = jnp.concatenate([mixer_pre[:, :, 1], state_pre], axis=2).astype(jnp.bfloat16)
    conv_weight = jnp.concatenate([conv_mixer, conv_state], axis=1)
    before = shifted(conv_input[:, length - (tap_count - 1) :], "seq", 1)
    padded = jnp.concatenate([before, conv_input], axis=1)
    conv_pre = jnp.zeros(conv_input.shape, jnp.float32)
    for tap_index in range(tap_count):
        lag_steps = tap_count - 1 - tap_index
        conv_pre = conv_pre + jnp.where(
            (positions >= lag_steps)[:, :, None],
            padded[:, tap_index : tap_index + length] * conv_weight[tap_index],
            0.0,
        )
    activated = silu_value(conv_pre).astype(jnp.bfloat16)
    mixer_act = (
        activated[:, :, :inner_width]
        .reshape(row_count, length, head_count, head_dim)
        .astype(jnp.float32)
    )
    state_b = activated[:, :, inner_width : inner_width + states].astype(jnp.float32)
    state_c = activated[:, :, inner_width + states :].astype(jnp.float32)
    step_size = jax.nn.softplus(step_pre + step_bias)
    decay_rates = jnp.exp(decay_log)
    log_keep = -step_size * decay_rates
    (fresh_state, keep_rate), summary_back = jax.vjp(
        partial(state_summary, doc_ids, positions), mixer_act, state_b, step_size, log_keep
    )
    seq_index = lax.axis_index("seq")
    all_keep = lax.all_gather(keep_rate.astype(jnp.bfloat16), "seq")
    entering = carried_in(
        all_keep, lax.all_gather(fresh_state.astype(jnp.bfloat16), "seq"), seq_index, False
    )
    mixed_state, output_back = jax.vjp(
        partial(state_output, doc_ids, positions),
        mixer_act,
        state_b,
        state_c,
        step_size,
        log_keep,
        entering,
    )
    full_state = mixed_state + skip_gain[:, None] * mixer_act
    gated_low = (
        (full_state * silu_value(gate_view))
        .reshape(row_count, length, inner_width)
        .astype(jnp.bfloat16)
    )
    mixer_part = jnp.einsum(
        "rtc,cd->rtd", gated_low, mixer_down, preferred_element_type=jnp.float32
    )
    query_rot = rotate(
        query_pre.reshape(row_count, length, local_heads, ATT_DIM), positions, 1.0
    ).astype(jnp.bfloat16)
    key_rot = rotate(keyval_pre[:, :, 0][:, :, None], positions, 1.0)[:, :, 0].astype(jnp.bfloat16)
    value_low = keyval_pre[:, :, 1].astype(jnp.bfloat16)
    keyval_all = lax.all_gather(
        jnp.concatenate([key_rot, value_low], axis=2), "seq", axis=1, tiled=True
    )
    keyval_t = jnp.swapaxes(keyval_all, 1, 2)
    query_scaled = (
        jnp.swapaxes(query_rot, 1, 2).reshape(row_count, local_heads * length, ATT_DIM)
        * jnp.bfloat16(score_scale)
    )
    begins = offset + places[None, :] - positions
    place_row = jnp.tile(offset + places, local_heads)[None, None, :]
    place_row = jnp.broadcast_to(place_row, (row_count, 1, local_heads * length))
    begin_row = jnp.tile(begins, (1, local_heads))[:, None, :]
    low_block = begins[:, 0] // length
    high_block = jnp.broadcast_to(lax.axis_index("seq") + 1, (row_count,)).astype(jnp.int32)
    attended_t, stat_row = attend_forward(
        length, low_block, high_block, query_scaled, place_row, begin_row, keyval_all, keyval_t
    )
    attended = attended_t.reshape(row_count, ATT_DIM, local_heads, length).transpose(0, 3, 2, 1)
    attended_low = attended.astype(jnp.bfloat16).reshape(row_count, length, local_heads * ATT_DIM)
    attend_part = jnp.einsum(
        "rtc,cd->rtd", attended_low, attend_down, preferred_element_type=jnp.float32
    )
    mixed_sum = lax.psum((mixer_part + attend_part).astype(jnp.bfloat16), "head").astype(
        jnp.float32
    )
    middle = inputs + mixed_sum
    normed_two, scaled_two, gained_two = norm_forward(middle, ffn_gain)
    middle_low = gained_two.astype(jnp.bfloat16)
    ffn_pre = jnp.einsum("rtd,dkf->rtkf", middle_low, ffn_in, preferred_element_type=jnp.float32)
    hidden = (silu_value(ffn_pre[:, :, 0]) * ffn_pre[:, :, 1]).astype(jnp.bfloat16)
    ffn_part = jnp.einsum("rtf,fd->rtd", hidden, ffn_down, preferred_element_type=jnp.float32)
    ffn_share_sum = lax.psum_scatter(
        ffn_part.astype(jnp.bfloat16), "head", scatter_dimension=1, tiled=True
    ).astype(jnp.float32)
    output_share = (share_of(middle) + ffn_share_sum).astype(jnp.bfloat16)
    hidden_grad = jnp.einsum("rtd,fd->rtf", cotangent, ffn_down, preferred_element_type=jnp.float32)
    ffn_down_grad = jnp.einsum("rtf,rtd->fd", hidden, cotangent, preferred_element_type=jnp.float32)
    gate_value = ffn_pre[:, :, 0]
    ffn_pre_grad = jnp.stack(
        [
            hidden_grad * ffn_pre[:, :, 1] * silu_slope(gate_value),
            hidden_grad * silu_value(gate_value),
        ],
        axis=2,
    ).astype(jnp.bfloat16)
    ffn_in_grad = jnp.einsum(
        "rtd,rtkf->dkf", middle_low, ffn_pre_grad, preferred_element_type=jnp.float32
    )
    middle_low_part = jnp.einsum(
        "rtkf,dkf->rtd", ffn_pre_grad, ffn_in, preferred_element_type=jnp.float32
    )
    def tall(values):
        return jnp.pad(values, ((0, model_width - values.shape[0]), (0, 0)))

    early = jnp.concatenate(
        [ffn_in_grad.reshape(model_width, -1), ffn_down_grad.T], axis=1
    ).astype(jnp.bfloat16)
    middle_low_part, early = lax.optimization_barrier(
        (middle_low_part.astype(jnp.bfloat16), early)
    )
    low_grad_share = lax.psum_scatter(
        middle_low_part, "head", scatter_dimension=1, tiled=True
    )
    early_sum = grads_sum(early, 1)
    low_grad_share, early_sum = lax.optimization_barrier((low_grad_share, early_sum))
    low_grad_share = low_grad_share.astype(jnp.float32)
    norm_back_share, ffn_gain_part = norm_backward(
        low_grad_share, share_of(normed_two), share_of(scaled_two), ffn_gain
    )
    middle_grad_share = share_of(cotangent).astype(jnp.float32) + norm_back_share
    mixed_low = lax.all_gather(middle_grad_share.astype(jnp.bfloat16), "head", axis=1, tiled=True)
    gated_grad = jnp.einsum(
        "rtd,cd->rtc", mixed_low, mixer_down, preferred_element_type=jnp.float32
    ).reshape(row_count, length, head_count, head_dim)
    mixer_down_grad = jnp.einsum(
        "rtc,rtd->cd", gated_low, mixed_low, preferred_element_type=jnp.float32
    )
    attended_grad = jnp.einsum(
        "rtd,cd->rtc", mixed_low, attend_down, preferred_element_type=jnp.float32
    ).astype(jnp.bfloat16)
    attend_down_grad = jnp.einsum(
        "rtc,rtd->cd", attended_low, mixed_low, preferred_element_type=jnp.float32
    )
    attended_grad = attended_grad.reshape(row_count, length, local_heads, ATT_DIM)
    grad_dot = jnp.swapaxes(jnp.sum(attended_grad.astype(jnp.float32) * attended, axis=-1), 1, 2)

    query_grad_t, keyval_grads = attend_backward(
        length,
        low_block,
        high_block,
        query_scaled,
        jnp.swapaxes(attended_grad, 1, 2).reshape(row_count, local_heads * length, ATT_DIM),
        place_row,
        begin_row,
        stat_row,
        grad_dot.reshape(row_count, 1, local_heads * length),
        keyval_all,
        keyval_t,
    )
    query_grad = (
        query_grad_t.reshape(row_count, ATT_DIM, local_heads, length).transpose(0, 3, 2, 1)
        * score_scale
    )
    keyval_grad = lax.psum_scatter(
        keyval_grads, "seq", scatter_dimension=1, tiled=True
    ).astype(jnp.float32)
    key_grad, value_grad = keyval_grad[..., :ATT_DIM], keyval_grad[..., ATT_DIM:]
    query_low = (
        rotate(query_grad, positions, -1.0)
        .reshape(row_count, length, local_heads * ATT_DIM)
        .astype(jnp.bfloat16)
    )
    keyval_own = jnp.stack(
        [rotate(key_grad[:, :, None], positions, -1.0)[:, :, 0], value_grad], axis=2
    )
    keyval_part = jnp.zeros((row_count, length, 2, kv_total, ATT_DIM), jnp.float32)
    keyval_part = lax.dynamic_update_slice_in_dim(
        keyval_part, keyval_own[:, :, :, None], kv_index, 3
    )
    state_grad = gated_grad * silu_value(gate_view)
    gate_grad = gated_grad * full_state * silu_slope(gate_view)
    skip_gain_grad = jnp.sum(state_grad * mixer_act, axis=(0, 1, 3))
    lift_rate = jnp.where(
        (positions > places)[:, :, None], jnp.exp(running_sum(log_keep)), 0.0
    )
    local_grad = jnp.einsum(
        "rthp,rtn->rhpn", state_grad * lift_rate[..., None], state_c, precision=PRECISE
    )
    after_grad = carried_in(
        all_keep, lax.all_gather(local_grad.astype(jnp.bfloat16), "seq"), seq_index, True
    )
    keep_grad = jnp.sum(after_grad * entering, axis=(2, 3))
    act_grad_one, b_grad_one, step_grad_one, log_grad_one = summary_back((after_grad, keep_grad))
    act_grad_two, b_grad_two, c_grad, step_grad_two, log_grad_two, entering_grad = output_back(
        state_grad
    )
    mixer_act_grad = act_grad_one + act_grad_two + state_grad * skip_gain[:, None]
    log_grad = log_grad_one + log_grad_two
    step_grad = step_grad_one + step_grad_two - log_grad * decay_rates
    decay_log_grad = jnp.sum(log_grad * log_keep, axis=(0, 1))
    step_pre_grad = step_grad * jax.nn.sigmoid(step_pre + step_bias)
    step_bias_grad = jnp.sum(step_pre_grad, axis=(0, 1))
    step_low = step_pre_grad.astype(jnp.bfloat16)
    act_grad = jnp.concatenate(
        [mixer_act_grad.reshape(row_count, length, inner_width), b_grad_one + b_grad_two, c_grad],
        axis=2,
    )
    pre_grad = act_grad * silu_slope(conv_pre)
    state_total, keyval_total = (
        lax.psum(pre_grad[:, :, inner_width:].astype(jnp.bfloat16), "head").astype(jnp.float32),
        lax.psum(keyval_part.astype(jnp.bfloat16), "head").astype(jnp.float32),
    )
    pre_grad = jnp.concatenate([pre_grad[:, :, :inner_width], state_total], axis=2)
    padded_grad = jnp.zeros((row_count, length + tap_count - 1, pre_grad.shape[2]), jnp.float32)
    conv_grads = []
    for tap_index in range(tap_count):
        lag_steps = tap_count - 1 - tap_index
        masked = jnp.where((positions >= lag_steps)[:, :, None], pre_grad, 0.0)
        conv_grads.append(jnp.sum(masked * padded[:, tap_index : tap_index + length], axis=(0, 1)))
        padded_grad = padded_grad + jnp.pad(
            masked * conv_weight[tap_index], ((0, 0), (tap_index, lag_steps), (0, 0))
        )
    conv_weight_grad = jnp.stack(conv_grads, axis=0)
    rim_grad = shifted(padded_grad[:, : tap_count - 1], "seq", -1)
    conv_input_grad = padded_grad[:, tap_count - 1 :] + jnp.pad(
        rim_grad, ((0, 0), (length - (tap_count - 1), 0), (0, 0))
    )
    mixer_low = jnp.stack(
        [gate_grad.reshape(row_count, length, inner_width), conv_input_grad[:, :, :inner_width]],
        axis=2,
    ).astype(jnp.bfloat16)
    state_low = conv_input_grad[:, :, inner_width:].astype(jnp.bfloat16)
    keyval_low = keyval_total.reshape(row_count, length, 2, kv_total * ATT_DIM).astype(jnp.bfloat16)
    mixer_proj_grad = jnp.einsum(
        "rtd,rtkc->dkc", normed_low, mixer_low, preferred_element_type=jnp.float32
    )
    state_proj_grad = jnp.einsum(
        "rtd,rtc->dc", normed_low, state_low, preferred_element_type=jnp.float32
    )
    step_proj_grad = jnp.einsum(
        "rtd,rth->dh", normed_low, step_low, preferred_element_type=jnp.float32
    )
    query_proj_grad = jnp.einsum(
        "rtd,rtc->dc", normed_low, query_low, preferred_element_type=jnp.float32
    )
    keyval_proj_grad = jnp.einsum(
        "rtd,rtkc->dkc", normed_low, keyval_low, preferred_element_type=jnp.float32
    )
    head_part = (
        jnp.einsum("rtkc,dkc->rtd", mixer_low, mixer_proj, preferred_element_type=jnp.float32)
        + jnp.einsum("rth,dh->rtd", step_low, step_proj, preferred_element_type=jnp.float32)
        + jnp.einsum("rtc,dc->rtd", query_low, query_proj, preferred_element_type=jnp.float32)
    )
    common_share = jnp.einsum(
        "rtc,dc->rtd", share_of(state_low), state_proj, preferred_element_type=jnp.float32
    ) + jnp.einsum(
        "rtkc,dkc->rtd", share_of(keyval_low), keyval_proj, preferred_element_type=jnp.float32
    )
    normed_share = share_of(normed_one)
    norm_rider = jnp.sum(head_part * normed_one, axis=(0, 1)) + jnp.sum(
        common_share * normed_share, axis=(0, 1)
    )
    head_share, ffn_gain_total, norm_gain_total = (
        lax.psum_scatter(
            head_part.astype(jnp.bfloat16), "head", scatter_dimension=1, tiled=True
        ).astype(jnp.float32),
        lax.psum_scatter(
            jnp.broadcast_to(ffn_gain_part[None, None, :], (1, head_ways, model_width)).astype(
                jnp.bfloat16
            ),
            "head",
            scatter_dimension=1,
            tiled=True,
        ).astype(jnp.float32),
        lax.psum_scatter(
            jnp.broadcast_to(norm_rider[None, None, :], (1, head_ways, model_width)).astype(
                jnp.bfloat16
            ),
            "head",
            scatter_dimension=1,
            tiled=True,
        ).astype(jnp.float32),
    )
    ffn_gain_grad = ffn_gain_total.reshape(model_width)
    norm_gain_grad = norm_gain_total.reshape(model_width)
    norm_back_share_one, unused_gain = norm_backward(
        head_share + common_share, normed_share, share_of(scaled_one), norm_gain
    )
    token_share = (middle_grad_share + norm_back_share_one).astype(jnp.bfloat16)
    small = [
        step_proj_grad,
        jnp.stack([ffn_gain_grad, norm_gain_grad], axis=1),
        tall(conv_weight_grad[:, :inner_width].T),
        tall(conv_weight_grad[:, inner_width:].T),
        tall(jnp.stack([step_bias_grad, decay_log_grad, skip_gain_grad], axis=1)),
    ]
    small = jnp.concatenate(small, axis=1)
    small = jnp.pad(small, ((0, 0), (0, 128 - small.shape[1])))
    down_grads = [mixer_down_grad, attend_down_grad]
    pieces = [
        mixer_proj_grad.reshape(model_width, -1),
        query_proj_grad,
        state_proj_grad,
        keyval_proj_grad.reshape(model_width, -1),
        jnp.concatenate(down_grads, axis=0).T,
        small,
    ]
    late = jnp.concatenate([piece.astype(jnp.bfloat16) for piece in pieces], axis=1)
    token_share, late = lax.optimization_barrier((token_share, late))
    output, token_grad = (
        lax.all_gather(output_share, "head", axis=1, tiled=True),
        lax.all_gather(token_share, "head", axis=1, tiled=True),
    )
    summed = grads_sum(late, 2)
    parts = []
    begin = 0
    for piece in pieces:
        parts.append(summed[:, begin : begin + piece.shape[1]].astype(jnp.float32))
        begin += piece.shape[1]
    mixer_proj_sum = parts[0].reshape(mixer_proj_grad.shape)
    query_proj_sum, state_proj_sum = parts[1], parts[2]
    keyval_proj_sum = parts[3].reshape(keyval_proj_grad.shape)
    down_sum = parts[4].T
    mixer_down_sum, attend_down_sum = down_sum[:inner_width], down_sum[inner_width:]
    early_wide = ffn_in_grad.shape[1] * ffn_in_grad.shape[2]
    ffn_in_sum = early_sum[:, :early_wide].astype(jnp.float32).reshape(ffn_in_grad.shape)
    ffn_down_sum = early_sum[:, early_wide:].astype(jnp.float32).T
    small_sum = parts[5]
    at = head_count
    step_proj_sum = small_sum[:, :at]
    ffn_gain_sum, norm_gain_sum = small_sum[:, at], small_sum[:, at + 1]
    at += 2
    conv_mixer_sum = small_sum[:inner_width, at : at + tap_count].T
    at += tap_count
    conv_state_sum = small_sum[: 2 * states, at : at + tap_count].T
    at += tap_count
    step_bias_sum, decay_log_sum, skip_gain_sum = (small_sum[:head_count, at + i] for i in range(3))
    return (
        output,
        token_grad,
        norm_gain_sum,
        mixer_proj_sum,
        state_proj_sum,
        step_proj_sum,
        step_bias_sum,
        decay_log_sum,
        skip_gain_sum,
        conv_mixer_sum,
        conv_state_sum,
        mixer_down_sum,
        query_proj_sum,
        keyval_proj_sum,
        attend_down_sum,
        ffn_gain_sum,
        ffn_in_sum,
        ffn_down_sum,
    )


def solution(mesh):
    placed = (
        P(None, "seq", None),
        P(None, "seq", None),
        P(),
        P(),
        P(None, None, "head"),
        P(),
        P(None, "head"),
        P("head"),
        P("head"),
        P("head"),
        P(None, "head"),
        P(),
        P("head", None),
        P(None, "head"),
        P(),
        P("head", None),
        P(),
        P(None, None, "head"),
        P("head", None),
    )
    return jax.shard_map(
        local,
        mesh=mesh,
        in_specs=placed,
        out_specs=(
            P(None, "seq", None),
            P(None, "seq", None),
            P(),
            P(None, None, "head"),
            P(),
            P(None, "head"),
            P("head"),
            P("head"),
            P("head"),
            P(None, "head"),
            P(),
            P("head", None),
            P(None, "head"),
            P(),
            P("head", None),
            P(),
            P(None, None, "head"),
            P("head", None),
        ),
        check_vma=False,
    )
```
